32 devices in a mesh: dp: 4 (over y, x), head: 8 (over z, core).
Axes of the slice: x: 2, y: 2, z: 4, core: 2. Of those that a mesh axis runs over, the one named last changes fastest.
Arguments:
- hidden: bfloat16 [4, 512, 1024], P('dp', 'head'), may hold values from -6 to 6
- core_grad: bfloat16 [4, 512, 1024], P('dp', 'head'), may hold values from -4 to 4
- query_weight: bfloat16 [1024, 512], P(None, 'head'), may hold values from -0.1875 to 0.1875
- key_weight: bfloat16 [1024, 512], P(None, 'head'), may hold values from -0.1875 to 0.1875
- value_weight: bfloat16 [1024, 1024], P(None, 'head'), may hold values from -0.1875 to 0.1875
- beta_weight: bfloat16 [1024, 8], P(None, 'head'), may hold values from -0.1875 to 0.1875
- decay_weight: bfloat16 [1024, 8], P(None, 'head'), may hold values from -0.1875 to 0.1875
- decay_log: float32 [8], P('head'), may hold values from 0 to 2.7
- decay_bias: float32 [8], P('head'), may hold values from -6 to -1
Outputs:
- token_grad: bfloat16 [4, 512, 1024], P('dp', 'head')
- query_grad: float32 [1024, 512], P(None, 'head')
- key_grad: float32 [1024, 512], P(None, 'head')
- value_grad: float32 [1024, 1024], P(None, 'head')
The draws below stay inside these ranges and needn't reach their ends.
All inputs are finite; a program needn't handle non-finite values.
Results may differ from the reference program's by a relative error of at most 0.013.
Values may be sent and summed in bfloat16 or wider, within the bound.
No kernel may reach another device: no remote copies, remote signals or barrier semaphores. Data moves between devices by JAX's collectives and lax.ppermute only.
A program may use at most 128 MiB of HBM per device.

```python
import jax
import jax.numpy as jnp
from jax import lax

D = 1024
HDIM = 128
BLOCK = 64
LEN = 512
VHEADS = 8
QKHEADS = 4
SEQS = 4


def shard_levels(own_key, extent, split, smallest, high):
    def one(position, blocks):
        steps = jax.random.uniform(jax.random.fold_in(jax.random.fold_in(own_key, 6), position), (blocks,), jnp.float32, smallest / len(split), high / len(split))
        return jnp.repeat(jnp.exp(steps), extent[position] // blocks).reshape((-1,) + (1,) * (len(extent) - position - 1))

    factor_of = one(*split[0])
    for cut in split[1:]:
        factor_of = factor_of * one(*cut)
    return factor_of


def bell_draw(stream_key, extent, scale, bound, cuts=(), held_as=jnp.bfloat16):
    array = scale * jax.random.normal(stream_key, extent, jnp.float32)
    if cuts:
        array = array * shard_levels(stream_key, extent, cuts, -0.22, 0.18)
    return jnp.clip(array, -bound, bound).astype(held_as)


def setup_inputs(seed: int = 0) -> dict:
    arg_keys = jax.random.split(jax.random.key(seed), 10)
    return {
        "hidden": bell_draw(arg_keys[0], (SEQS, LEN, D), 1.0, 6.0, ((0, 4), (1, 8))),
        "core_grad": bell_draw(arg_keys[1], (SEQS, LEN, VHEADS * HDIM), 0.5, 4.0, ((0, 4), (1, 8))),
        "query_weight": bell_draw(arg_keys[2], (D, QKHEADS * HDIM), D ** -0.5, 0.1875, ((1, 8),)),
        "key_weight": bell_draw(arg_keys[3], (D, QKHEADS * HDIM), D ** -0.5, 0.1875, ((1, 8),)),
        "value_weight": bell_draw(arg_keys[4], (D, VHEADS * HDIM), D ** -0.5, 0.1875, ((1, 8),)),
        "beta_weight": bell_draw(arg_keys[5], (D, VHEADS), D ** -0.5, 0.1875, ((1, 8),)),
        "decay_weight": bell_draw(arg_keys[6], (D, VHEADS), D ** -0.5, 0.1875, ((1, 8),)),
        "decay_log": jnp.clip(2.7 * jax.random.uniform(arg_keys[7], (VHEADS,), jnp.float32) ** shard_levels(arg_keys[7], (VHEADS,), ((0, 8),), -0.2, 0.2), 0.0, 2.7),
        "decay_bias": jnp.clip(-6.0 + 5.0 * jax.random.uniform(arg_keys[8], (VHEADS,), jnp.float32) ** shard_levels(arg_keys[8], (VHEADS,), ((0, 8),), -0.2, 0.2), -6.0, -1.0),
    }


eps_norm = 1e-06

def exact_dot(left, right):
    return jnp.dot(left, right, precision=lax.Precision.HIGHEST)

def blockwise_core(queries, keys, values, betas, logdecay, span_rows):
    total_rows = queries.shape[0]
    feature = queries.shape[1]
    num_blocks = total_rows // span_rows
    lower_mask = jnp.tril(jnp.ones((span_rows, span_rows), dtype=bool))
    strict_mask = jnp.tril(jnp.ones((span_rows, span_rows), dtype=bool), -1)
    identity = jnp.eye(span_rows, dtype=queries.dtype)

    def advance(memory, block_in):
        q_blk, k_blk, v_blk, b_blk, g_blk = block_in
        cumulative = jnp.cumsum(g_blk)
        spread = cumulative[:, None] - cumulative[None, :]
        decay_ratio = jnp.where(lower_mask, jnp.exp(jnp.where(lower_mask, spread, 0.0)), 0.0)
        decay_now = jnp.exp(cumulative)
        mixing = jnp.where(strict_mask, b_blk[:, None] * decay_ratio * exact_dot(k_blk, k_blk.T), 0.0)
        target = b_blk[:, None] * (v_blk - decay_now[:, None] * exact_dot(k_blk, memory.T))
        fresh_vals = jax.scipy.linalg.solve_triangular(identity + mixing, target, lower=True, unit_diagonal=True)
        attend = decay_ratio * exact_dot(q_blk, k_blk.T)
        result = decay_now[:, None] * exact_dot(q_blk, memory.T) + exact_dot(attend, fresh_vals)
        tail_weight = jnp.exp(cumulative[-1] - cumulative)
        memory = jnp.exp(cumulative[-1]) * memory + exact_dot((fresh_vals * tail_weight[:, None]).T, k_blk)
        return (memory, result)
    block_inputs = (queries.reshape(num_blocks, span_rows, feature), keys.reshape(num_blocks, span_rows, feature), values.reshape(num_blocks, span_rows, feature), betas.reshape(num_blocks, span_rows), logdecay.reshape(num_blocks, span_rows))
    start_memory = jnp.zeros((feature, feature), queries.dtype)
    final_memory, outputs = lax.scan(advance, start_memory, block_inputs)
    return outputs.reshape(total_rows, feature)

def core_forward(query_pre, key_pre, value_pre, beta_pre, decay_pre, log_rate, rate_bias, span_rows):
    feature = query_pre.shape[1]
    queries = query_pre * lax.rsqrt(lax.optimization_barrier(jnp.sum(query_pre * query_pre, axis=1, keepdims=True)) + eps_norm) * feature ** (-0.5)
    keys = key_pre * lax.rsqrt(lax.optimization_barrier(jnp.sum(key_pre * key_pre, axis=1, keepdims=True)) + eps_norm)
    betas = jax.nn.sigmoid(beta_pre)
    logdecay = -jnp.exp(log_rate) * jax.nn.softplus(decay_pre + rate_bias)
    return blockwise_core(queries, keys, value_pre, betas, logdecay, span_rows)

def reference(hidden, core_grad, query_weight, key_weight, value_weight, beta_weight, decay_weight, decay_log, decay_bias):
    query_heads_w = jnp.repeat(query_weight.reshape(D, QKHEADS, HDIM), 2, axis=1).transpose(1, 0, 2)
    key_heads_w = jnp.repeat(key_weight.reshape(D, QKHEADS, HDIM), 2, axis=1).transpose(1, 0, 2)
    value_heads_w = value_weight.reshape(D, VHEADS, HDIM).transpose(1, 0, 2)
    beta_heads_w = beta_weight.T
    decay_heads_w = decay_weight.T

    def head_grads(q_head, k_head, v_head, b_head, a_head, log_head, bias_head, cot_head):

        def forward(q_in, k_in, v_in, b_in, a_in):
            return core_forward(q_in, k_in, v_in, b_in, a_in, log_head, bias_head, BLOCK)
        output, pull = jax.vjp(forward, q_head, k_head, v_head, b_head, a_head)
        return pull(cot_head)

    def one_sequence(totals, seq_in):
        rows, cotangent = seq_in
        query_pre = jnp.dot(rows.astype(jnp.float32), query_weight.astype(jnp.float32), preferred_element_type=jnp.float32).reshape(LEN, QKHEADS, HDIM)
        key_pre = jnp.dot(rows.astype(jnp.float32), key_weight.astype(jnp.float32), preferred_element_type=jnp.float32).reshape(LEN, QKHEADS, HDIM)
        value_pre = jnp.dot(rows.astype(jnp.float32), value_weight.astype(jnp.float32), preferred_element_type=jnp.float32).reshape(LEN, VHEADS, HDIM)
        beta_pre = jnp.dot(rows.astype(jnp.float32), beta_weight.astype(jnp.float32), preferred_element_type=jnp.float32)
        decay_pre = jnp.dot(rows.astype(jnp.float32), decay_weight.astype(jnp.float32), preferred_element_type=jnp.float32)
        query_rep = jnp.repeat(query_pre, 2, axis=1)
        key_rep = jnp.repeat(key_pre, 2, axis=1)
        cot_heads = cotangent.astype(jnp.float32).reshape(LEN, VHEADS, HDIM)
        grads = jax.vmap(head_grads, in_axes=(1, 1, 1, 1, 1, 0, 0, 1))(query_rep, key_rep, value_pre, beta_pre, decay_pre, decay_log, decay_bias, cot_heads)
        grad_q = grads[0].astype(jnp.bfloat16)
        grad_k = grads[1].astype(jnp.bfloat16)
        grad_v = grads[2].astype(jnp.bfloat16)
        grad_b = grads[3].astype(jnp.bfloat16)
        grad_a = grads[4].astype(jnp.bfloat16)

        def add_head(total, per_head):
            hq, hk, hv, hb, ha, wq_h, wk_h, wv_h, wb_h, wa_h = per_head
            term = jnp.dot(hq.astype(jnp.float32), wq_h.T.astype(jnp.float32), preferred_element_type=jnp.float32)
            term = term + jnp.dot(hk.astype(jnp.float32), wk_h.T.astype(jnp.float32), preferred_element_type=jnp.float32)
            term = term + jnp.dot(hv.astype(jnp.float32), wv_h.T.astype(jnp.float32), preferred_element_type=jnp.float32)
            term = term + jnp.dot(hb[:, None].astype(jnp.float32), wb_h[None, :].astype(jnp.float32), preferred_element_type=jnp.float32)
            term = term + jnp.dot(ha[:, None].astype(jnp.float32), wa_h[None, :].astype(jnp.float32), preferred_element_type=jnp.float32)
            rounded = lax.optimization_barrier(term.astype(jnp.bfloat16)).astype(jnp.float32)
            return (total + rounded, None)
        token_total, unused = lax.scan(add_head, jnp.zeros((LEN, D), jnp.float32), (grad_q, grad_k, grad_v, grad_b, grad_a, query_heads_w, key_heads_w, value_heads_w, beta_heads_w, decay_heads_w))
        q_flat = grad_q.transpose(1, 0, 2).reshape(LEN, VHEADS * HDIM)
        k_flat = grad_k.transpose(1, 0, 2).reshape(LEN, VHEADS * HDIM)
        v_flat = grad_v.transpose(1, 0, 2).reshape(LEN, VHEADS * HDIM)
        q_part = jnp.dot(rows.T.astype(jnp.float32), q_flat.astype(jnp.float32), preferred_element_type=jnp.float32).reshape(D, QKHEADS, 2, HDIM)
        k_part = jnp.dot(rows.T.astype(jnp.float32), k_flat.astype(jnp.float32), preferred_element_type=jnp.float32).reshape(D, QKHEADS, 2, HDIM)
        q_pair = (q_part[:, :, 0, :] + q_part[:, :, 1, :]).reshape(D, QKHEADS * HDIM)
        k_pair = (k_part[:, :, 0, :] + k_part[:, :, 1, :]).reshape(D, QKHEADS * HDIM)
        v_part = jnp.dot(rows.T.astype(jnp.float32), v_flat.astype(jnp.float32), preferred_element_type=jnp.float32)
        totals = (totals[0] + q_pair, totals[1] + k_pair, totals[2] + v_part)
        return (totals, token_total.astype(jnp.bfloat16))
    start = (jnp.zeros((D, QKHEADS * HDIM), jnp.float32), jnp.zeros((D, QKHEADS * HDIM), jnp.float32), jnp.zeros((D, VHEADS * HDIM), jnp.float32))
    totals, token_grad = lax.scan(one_sequence, start, (hidden, core_grad))
    return (token_grad, totals[0] / SEQS, totals[1] / SEQS, totals[2] / SEQS)
```

```python
import jax
import jax.numpy as jnp
from jax import lax
from jax.experimental import pallas as pl
from jax.experimental.pallas import tpu as pltpu
from jax.sharding import PartitionSpec as P

CHUNK = 128
GROUP = 4
NORM_EPS = 1e-06
F32 = jnp.float32
BF16 = jnp.bfloat16


def nn(a, b):
    return lax.dot_general(a, b, (((1,), (0,)), ((), ())), preferred_element_type=F32)


def nt(a, b):
    return lax.dot_general(a, b, (((1,), (1,)), ((), ())), preferred_element_type=F32)


def tn(a, b):
    return lax.dot_general(a, b, (((0,), (0,)), ((), ())), preferred_element_type=F32)


def halves(a):
    high = a.astype(BF16)
    return high, (a - high.astype(F32)).astype(BF16)


def fine_nn(a, b):
    left = jnp.concatenate(a, 1)
    right = jnp.concatenate(b, 1)
    both = nn(left, jnp.concatenate([right, right], 0))
    width = b[0].shape[1]
    return both[:, :width] + both[:, width:]


def fine_gram(a):
    left = jnp.concatenate(a, 1)
    both = nt(left, jnp.concatenate([jnp.concatenate([p, p], 1) for p in a], 0))
    width = a[0].shape[0]
    return both[:, :width] + both[:, width:]


def row_sum(a):
    return jnp.sum(a, axis=1, keepdims=True)


def core_kernel(
    rows_ref, wq_ref, wq2_ref, wk_ref, wk2_ref, wv_ref, wb_ref, wa_ref, log_ref, bias_ref, cot_ref,
    out_ref,
    q_s, k_s, b_s, e_s, tail_s, gam_s, p_s, t_s, w_s, u0_s, kt_s, x_s, qn_s, kn_s,
    f_s, g_s, h_s, ec_s, m_s, d_s,
):
    total, head = cot_ref.shape
    num = total // CHUNK
    group = min(GROUP, num)
    scale = head ** -0.5
    row_id = lax.broadcasted_iota(jnp.int32, (CHUNK, CHUNK), 0)
    col_id = lax.broadcasted_iota(jnp.int32, (CHUNK, CHUNK), 1)
    low = row_id >= col_id
    strict = row_id > col_id
    low_ones = jnp.where(low, 1.0, 0.0).astype(BF16)
    high_ones = jnp.where(row_id <= col_id, 1.0, 0.0).astype(BF16)
    rate = -jnp.exp(log_ref[...])
    bias = bias_ref[...]

    def loop(body):
        if num == group:
            body(0)
        else:
            lax.fori_loop(0, num // group, lambda i, c: (body(i * group), c)[1], 0)

    def at(first, i):
        if isinstance(first, int):
            return pl.ds((first + i) * CHUNK, CHUNK)
        return pl.ds(pl.multiple_of((first + i) * CHUNK, CHUNK), CHUNK)

    features = wv_ref.shape[0]
    narrow = jnp.concatenate(
        [wq_ref[...], wq2_ref[...], wk_ref[...], wk2_ref[...],
         jnp.broadcast_to(wb_ref[...], (head, features)), jnp.broadcast_to(wa_ref[...], (head, features))], 0)

    def prepare(first):
        each = range(group)
        spans = [at(first, i) for i in each]
        mats, kparts, ek_bv = [], [], []
        for i in each:
            rows = rows_ref[spans[i], :]
            pre = nt(rows, narrow)
            v = nn(rows, wv_ref[...])
            qp, kp = pre[:, :head], pre[:, head : 2 * head]
            qn = lax.rsqrt(row_sum(qp * qp) + NORM_EPS)
            kn = lax.rsqrt(row_sum(kp * kp) + NORM_EPS)
            q = qp * (qn * scale)
            k = kp * kn
            beta = 1.0 / (1.0 + jnp.exp(-pre[:, 2 * head : 3 * head]))
            x = pre[:, 3 * head :] + bias
            g = rate * (jnp.maximum(x, 0.0) + jnp.log1p(jnp.exp(-jnp.abs(x))))
            g1 = g.astype(BF16)
            rest = g - g1.astype(F32)
            g2, g3 = halves(rest)
            sums = nn(low_ones, jnp.concatenate([g1, g2, g3], 1))
            c = sums[:, :head] + (sums[:, head : 2 * head] + sums[:, 2 * head :])
            last = c[CHUNK - 1 : CHUNK, :]
            e = jnp.exp(c)
            tail = jnp.exp(last - c)
            gam = jnp.exp(jnp.where(low, c - c.T, -1e30))
            kpair = halves(k)
            kk = fine_gram(kpair)
            qk = nt(q.astype(BF16), kpair[0])
            a = jnp.where(strict, beta * gam * kk, 0.0)
            p = (gam * qk).astype(BF16)
            kt = (tail * k).astype(BF16)
            q_s[spans[i], :] = q
            k_s[spans[i], :] = k
            b_s[spans[i], :] = beta
            e_s[spans[i], :] = e
            tail_s[spans[i], :] = tail
            gam_s[spans[i], :] = gam
            x_s[spans[i], :] = x
            p_s[spans[i], :] = p
            kt_s[spans[i], :] = kt
            qn_s[spans[i], :] = jnp.broadcast_to(qn * scale, (CHUNK, head))
            kn_s[spans[i], :] = jnp.broadcast_to(kn, (CHUNK, head))
            ec_s[first + i] = jnp.exp(jnp.broadcast_to(last, (8, head)))
            mats.append(a)
            ek_bv.append(jnp.concatenate([beta * e * k, beta * v], 1))
        eye = jnp.where(row_id == col_id, 1.0, 0.0)
        inv = [eye - jnp.where((row_id >> 1) == (col_id >> 1), a, 0.0) for a in mats]
        pairs = [halves(a) for a in mats]
        level = 1
        while (2 << level) <= CHUNK:
            joint = ((row_id >> (level + 1)) == (col_id >> (level + 1))) & ((row_id >> level) > (col_id >> level))
            tp = [halves(t) for t in inv]
            left = [
                fine_nn(tp[i], tuple(jnp.where(joint, half, jnp.zeros_like(half)) for half in pairs[i]))
                for i in each
            ]
            lp = [halves(z) for z in left]
            inv = [inv[i] - fine_nn(lp[i], tp[i]) for i in each]
            level += 1
        for i in each:
            tp = halves(inv[i])
            t_s[spans[i], :] = tp[0]
            ep = halves(ek_bv[i])
            wu = nn(jnp.concatenate(tp, 1), jnp.concatenate([ep[0], ep[0]], 0)) + nn(tp[0], ep[1])
            w = wu[:, :head].astype(BF16)
            w_s[spans[i], :] = w
            u0_s[spans[i], :] = wu[:, head:]
            fg = tn(kt_s[spans[i], :], jnp.concatenate([w, wu[:, head:].astype(BF16)], 1))
            f_s[spans[i], :] = fg[:, :head].astype(BF16)
            g_s[spans[i], :] = fg[:, head:]
            pw = nn(p_s[spans[i], :], w)
            h_s[spans[i], :] = tn((e_s[spans[i], :] * q_s[spans[i], :] - pw).astype(BF16), cot_ref[spans[i], :])

    loop(prepare)

    m_s[pl.ds(0, head), :] = jnp.zeros((head, head), F32)
    d_s[pl.ds((num - 1) * head, head), :] = jnp.zeros((head, head), F32)
    m = jnp.zeros((head, head), F32)
    d = jnp.zeros((head, head), F32)
    for i in range(num):
        span = pl.ds(i * CHUNK, CHUNK)
        if i == 0:
            m = g_s[span, :]
        else:
            m = ec_s[i][:1] * m - nn(f_s[span, :], m.astype(BF16)) + g_s[span, :]
        m_s[pl.ds((i + 1) * head, head), :] = m
        r = num - 1 - i
        if r > 0:
            back = pl.ds(r * CHUNK, CHUNK)
            if r == num - 1:
                d = h_s[back, :]
            else:
                d = ec_s[r][:1] * d - tn(f_s[back, :], d.astype(BF16)) + h_s[back, :]
            d_s[pl.ds((r - 1) * head, head), :] = d

    def finish(first):
        for i in range(group):
            span = at(first, i)
            nxt = at(first, i + 1)
            q, k, beta = q_s[span, :], k_s[span, :], b_s[span, :]
            gam, e, tail = gam_s[span, :], e_s[span, :], tail_s[span, :]
            do = cot_ref[span, :]
            m, d = m_s[span, :].astype(BF16), d_s[span, :]
            d16 = d.astype(BF16)
            q16, k16 = q.astype(BF16), k.astype(BF16)
            u = u0_s[span, :] - nn(w_s[span, :], m)
            u16 = u.astype(BF16)
            du = tn(p_s[span, :], do) + nn(kt_s[span, :], d16)
            dr = tn(t_s[span, :], du.astype(BF16))
            dv = beta * dr
            stacked = jnp.concatenate([do, dv.astype(BF16)], 0)
            wide = nt(stacked, jnp.concatenate([u16, m], 0))
            y = (wide[:CHUNK, :CHUNK] * gam).astype(BF16)
            x = jnp.where(strict, wide[CHUNK:, :CHUNK] * gam, 0.0).astype(BF16)
            yx = jnp.concatenate([y, x], 0)
            by_k = nn(yx, k16)
            dq = e * wide[:CHUNK, CHUNK:] + by_k[:CHUNK]
            dkr = -(e * wide[CHUNK:, CHUNK:] + by_k[CHUNK:])
            dkw = tail * nt(u16, d16) + tn(yx, jnp.concatenate([q16, -k16], 0))
            qdq = q * dq
            z = halves(qdq + k * (dkr - dkw))
            sums = nn(high_ones, jnp.concatenate(z, 1))
            dg = row_sum(sums[:, :head] + sums[:, head:]) + jnp.sum(m_s[nxt, :] * d)
            xs = x_s[span, :]
            ga = (dg * rate) * (1.0 / (1.0 + jnp.exp(-xs)))
            gb = row_sum(dr * u) * (1.0 - beta)
            dk = dkr + dkw
            out_ref[span, 0:head] = (qn_s[span, :] * (dq - q * (row_sum(qdq) * head))).astype(BF16)
            out_ref[span, head : 2 * head] = (kn_s[span, :] * (dk - k * row_sum(k * dk))).astype(BF16)
            out_ref[span, 2 * head : 3 * head] = dv.astype(BF16)
            lane = lax.broadcasted_iota(jnp.int32, (CHUNK, head), 1)
            out_ref[span, 3 * head :] = jnp.where(lane == 0, gb, jnp.where(lane == 1, ga, 0.0)).astype(BF16)

    loop(finish)


def core_grads(rows, wq, wq2, wk, wk2, wv, wb, wa, log_rate, rate_bias, cot):
    total, head = cot.shape
    num = total // CHUNK
    col = lambda dt: pltpu.VMEM((total, head), dt)
    states = pltpu.VMEM(((num + 1) * head, head), F32)
    return pl.pallas_call(
        core_kernel,
        out_shape=jax.ShapeDtypeStruct((total, 4 * head), BF16),
        in_specs=[pl.BlockSpec(memory_space=pltpu.VMEM)] * 11,
        out_specs=pl.BlockSpec(memory_space=pltpu.VMEM),
        scratch_shapes=[
            col(F32), col(F32), col(F32), col(F32), col(F32), col(F32), col(BF16), col(BF16), col(BF16), col(F32),
            col(BF16), col(F32), col(F32), col(F32),
            col(BF16), col(F32), col(F32), pltpu.VMEM((num, 8, head), F32), states, states,
        ],
        compiler_params=pltpu.CompilerParams(vmem_limit_bytes=48 * 1024 * 1024),
        name="core_grads",
    )(rows, wq, wq2, wk, wk2, wv, wb, wa, log_rate, rate_bias, cot)


def partner(block, axis):
    count = lax.axis_size(axis)
    return lax.ppermute(block, axis, [(i, i ^ 1) for i in range(count)])


def body(
    hidden, core_grad, query_weight, key_weight, value_weight, beta_weight, decay_weight, decay_log, decay_bias,
):
    half = query_weight.shape[1]
    head = value_weight.shape[1]
    devices = lax.axis_size("head")
    span = hidden.shape[1]
    wq, wk = query_weight.T, key_weight.T
    wq2, wk2 = partner((wq, wk), "head")
    cot = lax.all_to_all(
        core_grad[0].reshape(span, devices, head).transpose(1, 0, 2), "head", split_axis=0, concat_axis=0
    ).reshape(devices * span, head)
    rows = lax.all_gather(hidden[0], "head", axis=0, tiled=True)
    wb, wa = beta_weight.T, decay_weight.T
    grads = core_grads(
        rows, wq, wq2, wk, wk2, value_weight, wb, wa, decay_log.reshape(1, 1), decay_bias.reshape(1, 1), cot
    )
    gq, gk, gv, gba = jnp.split(grads, 4, axis=1)
    dot = lambda a, b, dims: lax.dot_general(a, b, (dims, ((), ())), preferred_element_type=jnp.float32)
    whole_weights = jnp.concatenate([wq, wq2, wk, wk2, value_weight.T, wb, wa], 0)
    term = dot(grads[:, : whole_weights.shape[0]], whole_weights, ((1,), (0,))).astype(jnp.bfloat16)
    token = lax.psum_scatter(term, "head", scatter_dimension=0, tiled=True)
    by_qk = dot(grads[:, : 2 * head], rows, ((0,), (0,)))
    value_sum = dot(rows, gv, ((0,), (0,))).astype(jnp.bfloat16)
    away = jnp.concatenate([by_qk[half:head], by_qk[head + half :]], 0).astype(jnp.bfloat16)
    near = jnp.concatenate([by_qk[:half], by_qk[head : head + half]], 0)
    qk_sum = (near + partner(away, "head").astype(jnp.float32)).astype(jnp.bfloat16)
    qk_total, value_total = lax.psum((qk_sum, value_sum), "dp")
    count = lax.axis_size("dp")
    qk_mean = qk_total.astype(jnp.float32) / count
    return token[None], qk_mean[:half].T, qk_mean[half:].T, value_total.astype(jnp.float32) / count


def solution(mesh):
    rows = P("dp", "head", None)
    cols = P(None, "head")
    return jax.shard_map(
        body,
        mesh=mesh,
        in_specs=(rows, rows, cols, cols, cols, cols, cols, P("head"), P("head")),
        out_specs=(rows, cols, cols, cols),
        check_vma=False,
    )
```

```python
import functools

import jax
import jax.numpy as jnp
from jax import lax
from jax.experimental import pallas as pl
from jax.experimental.pallas import tpu as pltpu
from jax.sharding import PartitionSpec as P

CHUNK = 128
GROUP = 4
NORM_EPS = 1e-06
F32 = jnp.float32
BF16 = jnp.bfloat16


def nn(a, b):
    return lax.dot_general(a, b, (((1,), (0,)), ((), ())), preferred_element_type=F32)


def nt(a, b):
    return lax.dot_general(a, b, (((1,), (1,)), ((), ())), preferred_element_type=F32)


def tn(a, b):
    return lax.dot_general(a, b, (((0,), (0,)), ((), ())), preferred_element_type=F32)


def halves(a):
    high = a.astype(BF16)
    return high, (a - high.astype(F32)).astype(BF16)


def fine_nn(a, b):
    left = jnp.concatenate(a, 1)
    right = jnp.concatenate(b, 1)
    both = nn(left, jnp.concatenate([right, right], 0))
    width = b[0].shape[1]
    return both[:, :width] + both[:, width:]


def fine_gram(a):
    left = jnp.concatenate(a, 1)
    both = nt(left, jnp.concatenate([jnp.concatenate([p, p], 1) for p in a], 0))
    width = a[0].shape[0]
    return both[:, :width] + both[:, width:]


def row_sum(a):
    return jnp.sum(a, axis=1, keepdims=True)


def core_kernel(
    chips,
    *refs,
):
    inputs, refs = refs[: 2 * chips], refs[2 * chips :]
    (
        wq_ref, wq2_ref, wk_ref, wk2_ref, wv_ref, wb_ref, wa_ref, log_ref, bias_ref,
        rows_ref, near_ref, away_ref, vsum_ref, mine_ref, theirs_ref,
        cot_ref, value_ref, kk_s, qk_s, q_s, k_s, b_s, e_s, tail_s, gam_s, p_s, t_s, w_s, u0_s, kt_s, x_s, qn_s, kn_s,
        f_s, g_s, h_s, ec_s, m_s, d_s,
    ) = refs
    place = lax.axis_index("head")
    core, chip = lax.rem(place, 2), place // 2
    part = inputs[0].shape[0]
    features, head = rows_ref.shape[1], cot_ref.shape[1]
    column = pl.ds(pl.multiple_of(features + core * head, head), head)
    for far in range(chips):
        for other in range(2):
            who = 2 * (chip ^ far) + (core ^ other)
            span = pl.ds(pl.multiple_of(who * part, part), part)
            message = inputs[2 * far + other]
            rows_ref[span, :] = message[:, :features]
            cot_ref[span, :] = message[:, column]
    total = cot_ref.shape[0]
    num = total // CHUNK
    group = min(GROUP, num)
    scale = head ** -0.5
    row_id = lax.broadcasted_iota(jnp.int32, (CHUNK, CHUNK), 0)
    col_id = lax.broadcasted_iota(jnp.int32, (CHUNK, CHUNK), 1)
    low = row_id >= col_id
    strict = row_id > col_id
    low_ones = jnp.where(low, 1.0, 0.0).astype(BF16)
    high_ones = jnp.where(row_id <= col_id, 1.0, 0.0).astype(BF16)
    below_ones = jnp.where(strict, 1.0, 0.0).astype(BF16)
    rate = -jnp.exp(log_ref[...])
    bias = bias_ref[...]

    def loop(body):
        if num == group:
            body(0)
        else:
            lax.fori_loop(0, num // group, lambda i, c: (body(i * group), c)[1], 0)

    def at(first, i):
        if isinstance(first, int):
            return pl.ds((first + i) * CHUNK, CHUNK)
        return pl.ds(pl.multiple_of((first + i) * CHUNK, CHUNK), CHUNK)

    narrow = jnp.concatenate(
        [wq_ref[...], wq2_ref[...], wk_ref[...], wk2_ref[...],
         jnp.broadcast_to(wb_ref[...], (head, features)), jnp.broadcast_to(wa_ref[...], (head, features))], 0)

    def prepare(first):
        each = range(group)
        spans = [at(first, i) for i in each]
        mats, kparts, ek_bv = [], [], []
        for i in each:
            rows = rows_ref[spans[i], :]
            pre = nt(rows, narrow)
            v = nn(rows, wv_ref[...])
            qp, kp = pre[:, :head], pre[:, head : 2 * head]
            qn = lax.rsqrt(row_sum(qp * qp) + NORM_EPS)
            kn = lax.rsqrt(row_sum(kp * kp) + NORM_EPS)
            q = qp * (qn * scale)
            k = kp * kn
            beta = 1.0 / (1.0 + jnp.exp(-pre[:, 2 * head : 3 * head]))
            x = pre[:, 3 * head :] + bias
            g = rate * (jnp.maximum(x, 0.0) + jnp.log1p(jnp.exp(-jnp.abs(x))))
            g1 = g.astype(BF16)
            rest = g - g1.astype(F32)
            g2, g3 = halves(rest)
            sums = nn(low_ones, jnp.concatenate([g1, g2, g3], 1))
            c = sums[:, :head] + (sums[:, head : 2 * head] + sums[:, 2 * head :])
            last = c[CHUNK - 1 : CHUNK, :]
            e = jnp.exp(c)
            tail = jnp.exp(last - c)
            gam = jnp.exp(jnp.where(low, c - c.T, -1e30))
            kpair = halves(k)
            kk = fine_gram(kpair)
            qk = nt(q.astype(BF16), kpair[0])
            a = jnp.where(strict, beta * gam * kk, 0.0)
            p = (gam * qk).astype(BF16)
            kt = (tail * k).astype(BF16)
            kk_s[spans[i], :] = kk
            qk_s[spans[i], :] = qk
            q_s[spans[i], :] = q
            k_s[spans[i], :] = k
            b_s[spans[i], :] = beta
            e_s[spans[i], :] = e
            tail_s[spans[i], :] = tail
            gam_s[spans[i], :] = gam
            x_s[spans[i], :] = x
            p_s[spans[i], :] = p
            kt_s[spans[i], :] = kt
            qn_s[spans[i], :] = jnp.broadcast_to(qn * scale, (CHUNK, head))
            kn_s[spans[i], :] = jnp.broadcast_to(kn, (CHUNK, head))
            ec_s[first + i] = jnp.exp(jnp.broadcast_to(last, (8, head)))
            mats.append(a)
            ek_bv.append(jnp.concatenate([beta * e * k, beta * v], 1))
        eye = jnp.where(row_id == col_id, 1.0, 0.0)
        inv = [eye - jnp.where((row_id >> 1) == (col_id >> 1), a, 0.0) for a in mats]
        pairs = [halves(a) for a in mats]
        level = 1
        while (2 << level) <= CHUNK:
            joint = ((row_id >> (level + 1)) == (col_id >> (level + 1))) & ((row_id >> level) > (col_id >> level))
            tp = [halves(t) for t in inv]
            left = [
                fine_nn(tp[i], tuple(jnp.where(joint, half, jnp.zeros_like(half)) for half in pairs[i]))
                for i in each
            ]
            lp = [halves(z) for z in left]
            inv = [inv[i] - fine_nn(lp[i], tp[i]) for i in each]
            level += 1
        for i in each:
            tp = halves(inv[i])
            t_s[spans[i], :] = tp[0]
            ep = halves(ek_bv[i])
            wu = nn(jnp.concatenate(tp, 1), jnp.concatenate([ep[0], ep[0]], 0)) + nn(tp[0], ep[1])
            w = wu[:, :head].astype(BF16)
            w_s[spans[i], :] = w
            u0_s[spans[i], :] = wu[:, head:]
            fg = tn(kt_s[spans[i], :], jnp.concatenate([w, wu[:, head:].astype(BF16)], 1))
            f_s[spans[i], :] = fg[:, :head].astype(BF16)
            g_s[spans[i], :] = fg[:, head:]
            pw = nn(p_s[spans[i], :], w)
            h_s[spans[i], :] = tn((e_s[spans[i], :] * q_s[spans[i], :] - pw).astype(BF16), cot_ref[spans[i], :])

    loop(prepare)

    m_s[pl.ds(0, head), :] = jnp.zeros((head, head), F32)
    d_s[pl.ds((num - 1) * head, head), :] = jnp.zeros((head, head), F32)
    m = jnp.zeros((head, head), F32)
    d = jnp.zeros((head, head), F32)
    for i in range(num):
        span = pl.ds(i * CHUNK, CHUNK)
        if i == 0:
            m = g_s[span, :]
        else:
            m = ec_s[i][:1] * m - nn(f_s[span, :], m.astype(BF16)) + g_s[span, :]
        m_s[pl.ds((i + 1) * head, head), :] = m
        r = num - 1 - i
        if r > 0:
            back = pl.ds(r * CHUNK, CHUNK)
            if r == num - 1:
                d = h_s[back, :]
            else:
                d = ec_s[r][:1] * d - tn(f_s[back, :], d.astype(BF16)) + h_s[back, :]
            d_s[pl.ds((r - 1) * head, head), :] = d

    def finish(first):
        for i in range(group):
            span = at(first, i)
            nxt = at(first, i + 1)
            q, k, beta = q_s[span, :], k_s[span, :], b_s[span, :]
            gam, e, tail = gam_s[span, :], e_s[span, :], tail_s[span, :]
            do = cot_ref[span, :]
            m, d = m_s[span, :].astype(BF16), d_s[span, :]
            d16 = d.astype(BF16)
            q16, k16 = q.astype(BF16), k.astype(BF16)
            u = u0_s[span, :] - nn(w_s[span, :], m)
            u16 = u.astype(BF16)
            du = tn(p_s[span, :], do) + nn(kt_s[span, :], d16)
            dr = tn(t_s[span, :], du.astype(BF16))
            dv = beta * dr
            stacked = jnp.concatenate([do, dv.astype(BF16)], 0)
            wide = nt(stacked, jnp.concatenate([u16, m], 0))
            y32 = wide[:CHUNK, :CHUNK] * gam
            x32 = jnp.where(strict, wide[CHUNK:, :CHUNK] * gam, 0.0)
            yx = jnp.concatenate([y32.astype(BF16), x32.astype(BF16)], 0)
            by_k = nn(yx, k16)
            from_q = e * wide[:CHUNK, CHUNK:]
            from_k = e * wide[CHUNK:, CHUNK:]
            to_k = tail * nt(u16, d16)
            dq = from_q + by_k[:CHUNK]
            dk = to_k - from_k - by_k[CHUNK:] + tn(yx, jnp.concatenate([q16, -k16], 0))
            zc = halves(jnp.where(strict, y32 * qk_s[span, :], 0.0) - x32 * kk_s[span, :])
            zr = halves(q * from_q - k * from_k)
            zt = halves(k * to_k)
            up = nn(high_ones, jnp.concatenate([*zc, *zr], 1))
            down = nn(below_ones, jnp.concatenate(zt, 1))
            crossing = jnp.where(strict, up[:, :head] + up[:, head : 2 * head], 0.0)
            single = up[:, 2 * head : 3 * head] + up[:, 3 * head :] + down[:, :head] + down[:, head:]
            dg = row_sum(crossing + single) + jnp.sum(ec_s[first + i][:1] * m_s[span, :] * d)
            qdq = q * dq
            xs = x_s[span, :]
            ga = (dg * rate) * (1.0 / (1.0 + jnp.exp(-xs)))
            gb = row_sum(dr * u) * (1.0 - beta)
            gq = (qn_s[span, :] * (dq - q * (row_sum(qdq) * head))).astype(BF16)
            gk = (kn_s[span, :] * (dk - k * row_sum(k * dk))).astype(BF16)
            gv = dv.astype(BF16)
            lane = lax.broadcasted_iota(jnp.int32, (CHUNK, head), 1)
            gba = jnp.where(lane == 2 * core, gb, jnp.where(lane == 2 * core + 1, ga, 0.0)).astype(BF16)
            half = head // 2
            near_ref[span, :] = jnp.concatenate([gq[:, :half], gk[:, :half]], 1)
            away_ref[span, :] = jnp.concatenate([gq[:, half:], gk[:, half:]], 1)
            value_ref[span, :] = gv
            g_s2 = jnp.concatenate([gq, gk, gv, gba], 1)
            swapped = jnp.concatenate([gq[:, half:], gq[:, :half], gk[:, half:], gk[:, :half], gv, gba], 1)
            pieces = CHUNK // (2 * part)
            for j in range(pieces):
                lo = slice(2 * j * part, (2 * j + 1) * part)
                hi = slice((2 * j + 1) * part, (2 * j + 2) * part)
                slot = (first + i) * pieces + j
                to = pl.ds(pl.multiple_of(slot * part, part), part)
                first_core = core == 0
                mine_ref[to, :] = jnp.where(first_core, g_s2[lo], g_s2[hi])
                theirs_ref[to, :] = jnp.where(first_core, swapped[hi], swapped[lo])

    loop(finish)
    vsum_ref[...] = tn(value_ref[...], rows_ref[...]).astype(BF16)


def core_grads(messages, wq, wq2, wk, wk2, wv, wb, wa, log_rate, rate_bias):
    part, features = messages[0].shape[0], wv.shape[0]
    head = wv.shape[1]
    total = part * len(messages)
    num = total // CHUNK
    col = lambda dt: pltpu.VMEM((total, head), dt)
    states = pltpu.VMEM(((num + 1) * head, head), F32)
    out = lambda rows, cols: jax.ShapeDtypeStruct((rows, cols), BF16)
    args = (*messages, wq, wq2, wk, wk2, wv, wb, wa, log_rate, rate_bias)
    return pl.pallas_call(
        functools.partial(core_kernel, len(messages) // 2),
        out_shape=(
            out(total, features), out(total, head), out(total, head), out(head, features),
            out(total // 2, 4 * head), out(total // 2, 4 * head),
        ),
        in_specs=[pl.BlockSpec(memory_space=pltpu.VMEM)] * len(args),
        out_specs=[pl.BlockSpec(memory_space=pltpu.VMEM)] * 6,
        scratch_shapes=[
            col(BF16), col(BF16), col(F32), col(F32),
            col(F32), col(F32), col(F32), col(F32), col(F32), col(F32), col(BF16), col(BF16), col(BF16), col(F32),
            col(BF16), col(F32), col(F32), col(F32),
            col(BF16), col(F32), col(F32), pltpu.VMEM((num, 8, head), F32), states, states,
        ],
        compiler_params=pltpu.CompilerParams(vmem_limit_bytes=48 * 1024 * 1024),
        name="core_grads",
    )(*args)


def pack_kernel(chips, hidden_ref, cot_ref, *outs):
    chip = lax.axis_index("head") // 2
    width, features = cot_ref.shape[1] // chips, hidden_ref.shape[1]
    for far, out in enumerate(outs):
        out[:, :features] = hidden_ref[...]
        out[:, features:] = cot_ref[:, pl.ds(pl.multiple_of((chip ^ far) * width, width), width)]


def product_kernel(
    part, rows_ref, near_ref, away_ref, mine_ref, recv_ref,
    wq_ref, wq2_ref, wk_ref, wk2_ref, wv_ref, wv2_ref, wb_ref, wa_ref, wb2_ref, wa2_ref, out_ref, *outs
):
    rows = rows_ref[...]
    out_ref[...] = (tn(near_ref[...], rows) + tn(away_ref[...], rows)).astype(BF16)
    place = lax.axis_index("head")
    core, chip = lax.rem(place, 2), place // 2
    head = wv_ref.shape[1]
    narrow = jnp.concatenate([wq_ref[...], wq2_ref[...], wk_ref[...], wk2_ref[...]], 0)
    features = narrow.shape[1]
    line = lax.broadcasted_iota(jnp.int32, (16, features), 0)
    small = jnp.zeros((16, features), F32)
    for offset, ref in ((2 * core, wb_ref), (2 * core + 1, wa_ref), (2 - 2 * core, wb2_ref), (3 - 2 * core, wa2_ref)):
        small = jnp.where(line == offset, ref[...].astype(F32), small)
    small = small.astype(BF16)
    for far, out in enumerate(outs):
        to = pl.ds(pl.multiple_of((chip ^ far) * part, part), part)
        mine, recv = mine_ref[to, :], recv_ref[to, :]
        both = nn(jnp.concatenate([mine[:, : 2 * head], recv[:, : 2 * head]], 1), jnp.concatenate([narrow, narrow], 0))
        both = both + nt(mine[:, 2 * head : 3 * head], wv_ref[...]) + nt(recv[:, 2 * head : 3 * head], wv2_ref[...])
        both = both + nn((mine[:, 3 * head :] + recv[:, 3 * head :])[:, :16], small)
        out[...] = both.astype(BF16)


def sum_kernel(*refs):
    total = refs[0][...].astype(F32)
    for ref in refs[1:-1]:
        total = total + ref[...].astype(F32)
    refs[-1][...] = total.astype(BF16)


def mean_kernel(count, own_qk, recv_qk, own_v, recv_v, q_ref, k_ref, v_ref):
    half = q_ref.shape[0]
    qk = (own_qk[...].astype(F32) + recv_qk[...].astype(F32)) * (1.0 / count)
    q_ref[...] = qk[:half]
    k_ref[...] = qk[half:]
    v_ref[...] = ((own_v[...].astype(F32) + recv_v[...].astype(F32)) * (1.0 / count)).T


def local_call(body, outs, args, name):
    many = isinstance(outs, tuple)
    spec = pl.BlockSpec(memory_space=pltpu.VMEM)
    return pl.pallas_call(
        body,
        out_shape=outs,
        in_specs=[spec] * len(args),
        out_specs=[spec] * len(outs) if many else spec,
        compiler_params=pltpu.CompilerParams(vmem_limit_bytes=48 * 1024 * 1024),
        name=name,
    )(*args)


def across(block, distance):
    count = lax.axis_size("head")
    return lax.ppermute(block, "head", [(i, i ^ distance) for i in range(count)])


def across_data(block, step):
    groups, places = lax.axis_size("dp"), lax.axis_size("head")
    bits = groups.bit_length() - 1
    route = []
    for g in range(groups):
        for p in range(places):
            bit = step if p % 2 == 0 else bits - 1 - step
            route.append((g * places + p, (g ^ (1 << bit)) * places + p))
    return lax.ppermute(block, ("dp", "head"), route)


def body(
    hidden, core_grad, query_weight, key_weight, value_weight, beta_weight, decay_weight, decay_log, decay_bias,
):
    half = query_weight.shape[1]
    head = value_weight.shape[1]
    chips = lax.axis_size("head") // 2
    part, features = hidden.shape[1:]
    order = sorted(range(1, chips), key=lambda d: -d)
    block = lambda rows, dt: jax.ShapeDtypeStruct((rows, features), dt)
    sent = local_call(
        functools.partial(pack_kernel, chips),
        (jax.ShapeDtypeStruct((part, features + 2 * head), BF16),) * chips, (hidden[0], core_grad[0]), "pack",
    )
    wq, wk = query_weight.T, key_weight.T
    wb, wa = beta_weight.T, decay_weight.T
    got = {d: across(sent[d], 2 * d) for d in order}
    got[0] = sent[0]
    messages = []
    for d in range(chips):
        messages += [got[d], across(got[d], 1)]
    wq2, wk2, wv2, wb2, wa2 = (across(w, 1) for w in (wq, wk, value_weight, wb, wa))

    all_rows, near, away, value, mine, theirs = core_grads(
        messages, wq, wq2, wk, wk2, value_weight, wb, wa, decay_log.reshape(1, 1), decay_bias.reshape(1, 1)
    )
    recv = across(away, 1)
    other = across(theirs, 1)
    qk, *terms = local_call(
        functools.partial(product_kernel, part), (block(head, BF16),) + (block(part, BF16),) * chips,
        (all_rows, near, recv, mine, other, wq, wq2, wk, wk2, value_weight, wv2, wb, wa, wb2, wa2), "products",
    )
    received = [across(terms[d], 2 * d) for d in order]
    groups = lax.axis_size("dp")
    rounds = groups.bit_length() - 1
    sums = {"value": value, "qk": qk}
    for step in range(rounds - 1):
        for name in sums:
            sums[name] = (sums[name].astype(F32) + across_data(sums[name], step).astype(F32)).astype(BF16)
    last = {name: across_data(sums[name], rounds - 1) for name in sums}
    token = local_call(sum_kernel, block(part, BF16), (terms[0], *received), "token_sum")
    q_mean, k_mean, v_mean = local_call(
        functools.partial(mean_kernel, groups),
        (block(half, F32), block(half, F32), jax.ShapeDtypeStruct((features, head), F32)),
        (sums["qk"], last["qk"], sums["value"], last["value"]), "weight_mean",
    )
    return token[None], q_mean.T, k_mean.T, v_mean


def solution(mesh):
    rows = P("dp", "head", None)
    cols = P(None, "head")
    return jax.shard_map(
        body,
        mesh=mesh,
        in_specs=(rows, rows, cols, cols, cols, cols, cols, P("head"), P("head")),
        out_specs=(rows, cols, cols, cols),
        check_vma=False,
    )
```

```python
import functools

import jax
import jax.numpy as jnp
from jax import lax
from jax.experimental import pallas as pl
from jax.experimental.pallas import tpu as pltpu
from jax.sharding import PartitionSpec as P

CHUNK = 128
GROUP = 4
NORM_EPS = 1e-06
F32 = jnp.float32
BF16 = jnp.bfloat16


def nn(a, b):
    return lax.dot_general(a, b, (((1,), (0,)), ((), ())), preferred_element_type=F32)


def nt(a, b):
    return lax.dot_general(a, b, (((1,), (1,)), ((), ())), preferred_element_type=F32)


def tn(a, b):
    return lax.dot_general(a, b, (((0,), (0,)), ((), ())), preferred_element_type=F32)


def halves(a):
    high = a.astype(BF16)
    return high, (a - high.astype(F32)).astype(BF16)


def fine_nn(a, b):
    left = jnp.concatenate(a, 1)
    right = jnp.concatenate(b, 1)
    both = nn(left, jnp.concatenate([right, right], 0))
    width = b[0].shape[1]
    return both[:, :width] + both[:, width:]


def fine_gram(a):
    left = jnp.concatenate(a, 1)
    both = nt(left, jnp.concatenate([jnp.concatenate([p, p], 1) for p in a], 0))
    width = a[0].shape[0]
    return both[:, :width] + both[:, width:]


def row_sum(a):
    return jnp.sum(a, axis=1, keepdims=True)


def core_kernel(
    order,
    *refs,
):
    inputs, refs = refs[: 2 * len(order)], refs[2 * len(order) :]
    (
        narrow_ref, narrow2_ref, wv_ref, log_ref, bias_ref,
        rows_ref, near_ref, away_ref, vsum_ref, mine_ref, theirs_ref,
        cot_ref, value_ref, kk_s, qk_s, q_s, k_s, b_s, e_s, tail_s, gam_s, p_s, t_s, w_s, u0_s, kt_s, x_s, qn_s, kn_s,
        f_s, g_s, h_s, ec_s, m_s, d_s,
    ) = refs
    place = lax.axis_index("head")
    core, chip = lax.rem(place, 2), place // 2
    part = inputs[0].shape[0]
    features, head = rows_ref.shape[1], cot_ref.shape[1]
    column = pl.ds(pl.multiple_of(features + core * head, head), head)
    for slot, far in enumerate(order):
        for other in range(2):
            who = 2 * (chip ^ far) + (core ^ other)
            span = pl.ds(pl.multiple_of(who * part, part), part)
            message = inputs[2 * slot + other]
            rows_ref[span, :] = message[:, :features]
            cot_ref[span, :] = message[:, column]
    total = cot_ref.shape[0]
    num = total // CHUNK
    group = min(GROUP, num)
    scale = head ** -0.5
    row_id = lax.broadcasted_iota(jnp.int32, (CHUNK, CHUNK), 0)
    col_id = lax.broadcasted_iota(jnp.int32, (CHUNK, CHUNK), 1)
    low = row_id >= col_id
    strict = row_id > col_id
    low_ones = jnp.where(low, 1.0, 0.0).astype(BF16)
    high_ones = jnp.where(row_id <= col_id, 1.0, 0.0).astype(BF16)
    below_ones = jnp.where(strict, 1.0, 0.0).astype(BF16)
    rate = -jnp.exp(log_ref[...])
    bias = bias_ref[...]

    def loop(body):
        if num == group:
            body(0)
        else:
            lax.fori_loop(0, num // group, lambda i, c: (body(i * group), c)[1], 0)

    def at(first, i):
        if isinstance(first, int):
            return pl.ds((first + i) * CHUNK, CHUNK)
        return pl.ds(pl.multiple_of((first + i) * CHUNK, CHUNK), CHUNK)

    half = head // 2
    own, partner = narrow_ref, narrow2_ref
    spread = lambda row: jnp.broadcast_to(own[pl.ds(head, 16), :][row : row + 1], (head, features))
    narrow = jnp.concatenate(
        [own[:half, :], partner[:half, :], own[half:head, :], partner[half:head, :], spread(0), spread(1)], 0)

    def rows_of(first):
        if isinstance(first, int):
            return pl.ds(first * CHUNK, group * CHUNK)
        return pl.ds(pl.multiple_of(first * CHUNK, CHUNK), group * CHUNK)

    each = range(group)
    cut = lambda a: [a[i * CHUNK : (i + 1) * CHUNK] for i in each]
    join = lambda parts: jnp.concatenate(parts, 0)

    def prepare(first):
        here = rows_of(first)
        spans = [at(first, i) for i in each]
        rows = rows_ref[here, :]
        pre = nt(rows, narrow)
        v = nn(rows, wv_ref[...])
        qp, kp = pre[:, :head], pre[:, head : 2 * head]
        qn = lax.rsqrt(row_sum(qp * qp) + NORM_EPS) * scale
        kn = lax.rsqrt(row_sum(kp * kp) + NORM_EPS)
        q = qp * qn
        k = kp * kn
        beta = 1.0 / (1.0 + jnp.exp(-pre[:, 2 * head : 3 * head]))
        x = pre[:, 3 * head :] + bias
        g = rate * (jnp.maximum(x, 0.0) + jnp.log1p(jnp.exp(-jnp.abs(x))))
        g1 = g.astype(BF16)
        g2, g3 = halves(g - g1.astype(F32))
        split = cut(jnp.concatenate([g1, g2, g3], 1))
        sums = [nn(low_ones, split[i]) for i in each]
        cs = [s[:, :head] + (s[:, head : 2 * head] + s[:, 2 * head :]) for s in sums]
        lasts = [c[CHUNK - 1 : CHUNK, :] for c in cs]
        e = jnp.exp(join(cs))
        tail = jnp.exp(join([last - c for last, c in zip(lasts, cs)]))
        gam = jnp.exp(join([jnp.where(low, c - c.T, -1e30) for c in cs]))
        kpair = halves(k)
        khigh, klow = cut(kpair[0]), cut(kpair[1])
        q16 = cut(q.astype(BF16))
        kk = join([fine_gram((khigh[i], klow[i])) for i in each])
        qk = join([nt(q16[i], khigh[i]) for i in each])
        strict_all, low_all = join([strict] * group), join([low] * group)
        mats = cut(jnp.where(strict_all, beta * gam * kk, 0.0))
        p_all = (gam * qk).astype(BF16)
        kt_all = (tail * k).astype(BF16)
        ek_bv = cut(jnp.concatenate([beta * e * k, beta * v], 1))
        p, kt, eq = cut(p_all), cut(kt_all), cut(e * q)
        for ref, value in (
            (kk_s, kk), (qk_s, qk), (q_s, q), (k_s, k), (b_s, beta), (e_s, e), (tail_s, tail), (gam_s, gam), (x_s, x),
            (p_s, p_all), (kt_s, kt_all),
            (qn_s, jnp.broadcast_to(qn, q.shape)), (kn_s, jnp.broadcast_to(kn, q.shape)),
        ):
            ref[here, :] = value
        for i in each:
            ec_s[first + i] = jnp.exp(jnp.broadcast_to(lasts[i], (8, head)))
        eye = jnp.where(row_id == col_id, 1.0, 0.0)
        inv = [eye - jnp.where((row_id >> 1) == (col_id >> 1), a, 0.0) for a in mats]
        pairs = [halves(a) for a in mats]
        level = 1
        while (2 << level) <= CHUNK:
            joint = ((row_id >> (level + 1)) == (col_id >> (level + 1))) & ((row_id >> level) > (col_id >> level))
            tp = [halves(t) for t in inv]
            left = [
                fine_nn(tp[i], tuple(jnp.where(joint, half, jnp.zeros_like(half)) for half in pairs[i]))
                for i in each
            ]
            lp = [halves(z) for z in left]
            inv = [inv[i] - fine_nn(lp[i], tp[i]) for i in each]
            level += 1
        tp = [halves(t) for t in inv]
        ep = [halves(y) for y in ek_bv]
        wu = [
            nn(jnp.concatenate(tp[i], 1), jnp.concatenate([ep[i][0], ep[i][0]], 0)) + nn(tp[i][0], ep[i][1])
            for i in each
        ]
        w = [y[:, :head].astype(BF16) for y in wu]
        fg = [tn(kt[i], jnp.concatenate([w[i], wu[i][:, head:].astype(BF16)], 1)) for i in each]
        pw = [nn(p[i], w[i]) for i in each]
        hs = [tn((eq[i] - pw[i]).astype(BF16), cot_ref[spans[i], :]) for i in each]
        t_s[here, :] = join([t[0] for t in tp])
        w_s[here, :] = join(w)
        u0_s[here, :] = join([y[:, head:] for y in wu])
        f_s[here, :] = join([y[:, :head].astype(BF16) for y in fg])
        g_s[here, :] = join([y[:, head:] for y in fg])
        h_s[here, :] = join(hs)

    loop(prepare)

    m_s[pl.ds(0, head), :] = jnp.zeros((head, head), F32)
    d_s[pl.ds((num - 1) * head, head), :] = jnp.zeros((head, head), F32)
    m = jnp.zeros((head, head), F32)
    d = jnp.zeros((head, head), F32)
    for i in range(num):
        span = pl.ds(i * CHUNK, CHUNK)
        if i == 0:
            m = g_s[span, :]
        else:
            m = ec_s[i][:1] * m - nn(f_s[span, :], m.astype(BF16)) + g_s[span, :]
        m_s[pl.ds((i + 1) * head, head), :] = m
        r = num - 1 - i
        if r > 0:
            back = pl.ds(r * CHUNK, CHUNK)
            if r == num - 1:
                d = h_s[back, :]
            else:
                d = ec_s[r][:1] * d - tn(f_s[back, :], d.astype(BF16)) + h_s[back, :]
            d_s[pl.ds((r - 1) * head, head), :] = d

    def finish(first):
        here = rows_of(first)
        q, k, beta = q_s[here, :], k_s[here, :], b_s[here, :]
        gam, e, tail = gam_s[here, :], e_s[here, :], tail_s[here, :]
        do = cot_ref[here, :]
        m32, d32 = m_s[here, :], d_s[here, :]
        m, d = cut(m32.astype(BF16)), cut(d32.astype(BF16))
        q16, k16 = q.astype(BF16), k.astype(BF16)
        k_parts, qk_parts = cut(k16), [join([a, b]) for a, b in zip(cut(q16), cut(-k16))]
        p, kt, t, w, dos = cut(p_s[here, :]), cut(kt_s[here, :]), cut(t_s[here, :]), cut(w_s[here, :]), cut(do)
        strict_all = join([strict] * group)
        du = [tn(p[i], dos[i]) + nn(kt[i], d[i]) for i in each]
        u = u0_s[here, :] - join([nn(w[i], m[i]) for i in each])
        u16 = cut(u.astype(BF16))
        dr = join([tn(t[i], du[i].astype(BF16)) for i in each])
        dv = beta * dr
        dv16 = dv.astype(BF16)
        dvs = cut(dv16)
        wide = [nt(join([dos[i], dvs[i]]), join([u16[i], m[i]])) for i in each]
        ud = join([nt(u16[i], d[i]) for i in each])
        y32 = join([a[:CHUNK, :CHUNK] for a in wide]) * gam
        x32 = jnp.where(strict_all, join([a[CHUNK:, :CHUNK] for a in wide]) * gam, 0.0)
        yx = [join([a, b]) for a, b in zip(cut(y32.astype(BF16)), cut(x32.astype(BF16)))]
        by_k = [nn(yx[i], k_parts[i]) for i in each]
        by_qk = join([tn(yx[i], qk_parts[i]) for i in each])
        from_q = e * join([a[:CHUNK, CHUNK:] for a in wide])
        from_k = e * join([a[CHUNK:, CHUNK:] for a in wide])
        to_k = tail * ud
        dq = from_q + join([a[:CHUNK] for a in by_k])
        dk = to_k - from_k - join([a[CHUNK:] for a in by_k]) + by_qk
        zc = halves(jnp.where(strict_all, y32 * qk_s[here, :], 0.0) - x32 * kk_s[here, :])
        zr = halves(q * from_q - k * from_k)
        zt = cut(jnp.concatenate(halves(k * to_k), 1))
        zs = cut(jnp.concatenate([*zc, *zr], 1))
        up = join([nn(high_ones, zs[i]) for i in each])
        down = join([nn(below_ones, zt[i]) for i in each])
        crossing = jnp.where(strict_all, up[:, :head] + up[:, head : 2 * head], 0.0)
        single = up[:, 2 * head : 3 * head] + up[:, 3 * head :] + down[:, :head] + down[:, head:]
        carried = join([
            jnp.broadcast_to(row_sum(jnp.sum(ec_s[first + i][:1] * a, axis=0, keepdims=True)), (CHUNK, 1))
            for i, a in enumerate(cut(m32 * d32))
        ])
        dg = row_sum(crossing + single) + carried
        ga = (dg * rate) * (1.0 / (1.0 + jnp.exp(-x_s[here, :])))
        gb = row_sum(dr * u) * (1.0 - beta)
        gq = (qn_s[here, :] * (dq - q * (row_sum(q * dq) * head))).astype(BF16)
        gk = (kn_s[here, :] * (dk - k * row_sum(k * dk))).astype(BF16)
        lane = lax.broadcasted_iota(jnp.int32, q.shape, 1)
        gba = jnp.where(lane == 0, gb, jnp.where(lane == 1, ga, 0.0)).astype(BF16)
        near_ref[here, :] = jnp.concatenate([gq[:, :half], gk[:, :half]], 1)
        away_ref[here, :] = jnp.concatenate([gq[:, half:], gk[:, half:]], 1)
        value_ref[here, :] = dv16
        forth = jnp.concatenate([gq, gk, dv16, gba], 1)
        swapped = jnp.concatenate([gq[:, half:], gq[:, :half], gk[:, half:], gk[:, :half], dv16, gba], 1)
        first_core = core == 0
        pieces = group * CHUNK // (2 * part)
        for j in range(pieces):
            lo = slice(2 * j * part, (2 * j + 1) * part)
            hi = slice((2 * j + 1) * part, (2 * j + 2) * part)
            slot = first * CHUNK // (2 * part) + j
            to = pl.ds(slot * part if isinstance(slot, int) else pl.multiple_of(slot * part, part), part)
            mine_ref[to, :] = jnp.where(first_core, forth[lo], forth[hi])
            theirs_ref[to, :] = jnp.where(first_core, swapped[hi], swapped[lo])

    loop(finish)
    vsum_ref[...] = tn(value_ref[...], rows_ref[...]).astype(BF16)


def core_grads(order, messages, narrow, narrow2, wv, log_rate, rate_bias):
    part, features = messages[0].shape[0], wv.shape[0]
    head = wv.shape[1]
    total = part * len(messages)
    num = total // CHUNK
    col = lambda dt: pltpu.VMEM((total, head), dt)
    states = pltpu.VMEM(((num + 1) * head, head), F32)
    out = lambda rows, cols: jax.ShapeDtypeStruct((rows, cols), BF16)
    args = (*messages, narrow, narrow2, wv, log_rate, rate_bias)
    return pl.pallas_call(
        functools.partial(core_kernel, order),
        out_shape=(
            out(total, features), out(total, head), out(total, head), out(head, features),
            out(total // 2, 4 * head), out(total // 2, 4 * head),
        ),
        in_specs=[pl.BlockSpec(memory_space=pltpu.VMEM)] * len(args),
        out_specs=[pl.BlockSpec(memory_space=pltpu.VMEM)] * 6,
        scratch_shapes=[
            col(BF16), col(BF16), col(F32), col(F32),
            col(F32), col(F32), col(F32), col(F32), col(F32), col(F32), col(BF16), col(BF16), col(BF16), col(F32),
            col(BF16), col(F32), col(F32), col(F32),
            col(BF16), col(F32), col(F32), pltpu.VMEM((num, 8, head), F32), states, states,
        ],
        compiler_params=pltpu.CompilerParams(vmem_limit_bytes=48 * 1024 * 1024),
        name="core_grads",
    )(*args)


def pack_kernel(chips, hidden_ref, cot_ref, *outs):
    chip = lax.axis_index("head") // 2
    width, features = cot_ref.shape[1] // chips, hidden_ref.shape[1]
    for far, out in enumerate(outs):
        out[:, :features] = hidden_ref[...]
        out[:, features:] = cot_ref[:, pl.ds(pl.multiple_of((chip ^ far) * width, width), width)]


def narrow_kernel(wq_ref, wk_ref, wb_ref, wa_ref, after_ref, out_ref):
    half, features = wq_ref.shape
    out_ref[pl.ds(0, half), :] = wq_ref[...]
    out_ref[pl.ds(half, half), :] = wk_ref[...]
    line = lax.broadcasted_iota(jnp.int32, (16, features), 0)
    beta, decay = wb_ref[...].astype(F32), wa_ref[...].astype(F32)
    out_ref[pl.ds(2 * half, 16), :] = jnp.where(line == 0, beta, jnp.where(line == 1, decay, 0.0)).astype(BF16)


def gram_kernel(rows_ref, near_ref, away_ref, out_ref):
    rows = rows_ref[...]
    out_ref[...] = (tn(near_ref[...], rows) + tn(away_ref[...], rows)).astype(BF16)


def term_kernel(part, mine_ref, recv_ref, own, partner, wv_ref, wv2_ref, *outs):
    chip = lax.axis_index("head") // 2
    head = wv_ref.shape[1]
    half = head // 2
    narrow = jnp.concatenate([own[:half, :], partner[:half, :], own[half:head, :], partner[half:head, :]], 0)
    small, small2 = own[pl.ds(head, 16), :], partner[pl.ds(head, 16), :]
    for far, out in enumerate(outs):
        to = pl.ds(pl.multiple_of((chip ^ far) * part, part), part)
        mine, recv = mine_ref[to, :], recv_ref[to, :]
        both = nn(jnp.concatenate([mine[:, : 2 * head], recv[:, : 2 * head]], 1), jnp.concatenate([narrow, narrow], 0))
        both = both + nt(mine[:, 2 * head : 3 * head], wv_ref[...]) + nt(recv[:, 2 * head : 3 * head], wv2_ref[...])
        both = both + nn(mine[:, 3 * head : 3 * head + 16], small) + nn(recv[:, 3 * head : 3 * head + 16], small2)
        out[...] = both.astype(BF16)


def sum_kernel(*refs):
    total = refs[0][...].astype(F32)
    for ref in refs[1:-1]:
        total = total + ref[...].astype(F32)
    refs[-1][...] = total.astype(BF16)


def mean_kernel(count, own_qk, recv_qk, own_v, recv_v, q_ref, k_ref, v_ref):
    half = q_ref.shape[0]
    qk = (own_qk[...].astype(F32) + recv_qk[...].astype(F32)) * (1.0 / count)
    q_ref[...] = qk[:half]
    k_ref[...] = qk[half:]
    v_ref[...] = ((own_v[...].astype(F32) + recv_v[...].astype(F32)) * (1.0 / count)).T


def add_kernel(own_ref, recv_ref, after_ref, out_ref):
    out_ref[...] = (own_ref[...].astype(F32) + recv_ref[...].astype(F32)).astype(BF16)


def local_call(body, outs, args, name, flops):
    many = isinstance(outs, tuple)
    spec = pl.BlockSpec(memory_space=pltpu.VMEM)
    return pl.pallas_call(
        body,
        out_shape=outs,
        in_specs=[spec] * len(args),
        out_specs=[spec] * len(outs) if many else spec,
        compiler_params=pltpu.CompilerParams(vmem_limit_bytes=48 * 1024 * 1024),
        cost_estimate=pl.CostEstimate(flops=flops, bytes_accessed=1 << 20, transcendentals=0),
        name=name,
    )(*args)


def across(block, distance):
    count = lax.axis_size("head")
    return lax.ppermute(block, "head", [(i, i ^ distance) for i in range(count)])


def across_data(block, step):
    groups, places = lax.axis_size("dp"), lax.axis_size("head")
    bits = groups.bit_length() - 1
    route = []
    for g in range(groups):
        for p in range(places):
            bit = step if p % 2 == 0 else bits - 1 - step
            route.append((g * places + p, (g ^ (1 << bit)) * places + p))
    return lax.ppermute(block, ("dp", "head"), route)


def body(
    hidden, core_grad, query_weight, key_weight, value_weight, beta_weight, decay_weight, decay_log, decay_bias,
):
    half = query_weight.shape[1]
    head = value_weight.shape[1]
    chips = lax.axis_size("head") // 2
    part, features = hidden.shape[1:]
    order = sorted(range(chips), key=lambda d: -d)
    block = lambda rows, dt: jax.ShapeDtypeStruct((rows, features), dt)
    message = jax.ShapeDtypeStruct((part, features + 2 * head), BF16)
    sent = local_call(
        functools.partial(pack_kernel, chips), (message,) * chips, (hidden[0], core_grad[0]), "pack", 1048576)
    got = {d: across(sent[d], 2 * d) if d else sent[0] for d in order}
    narrow = local_call(
        narrow_kernel, block(head + 16, BF16),
        (query_weight.T, key_weight.T, beta_weight.T, decay_weight.T, got[order[0]]), "narrow", 1048576)
    wv = value_weight
    messages = []
    for d in order:
        messages += [got[d], across(got[d], 1)]
    narrow2, wv2 = across(narrow, 1), across(wv, 1)

    all_rows, near, away, value, mine, theirs = core_grads(
        order, messages, narrow, narrow2, wv, decay_log.reshape(1, 1), decay_bias.reshape(1, 1))
    recv = across(away, 1)
    other = across(theirs, 1)
    qk = local_call(gram_kernel, block(head, BF16), (all_rows, near, recv), "gram", 268435456)
    terms = local_call(
        functools.partial(term_kernel, part), (block(part, BF16),) * chips,
        (mine, other, narrow, narrow2, wv, wv2), "terms", 1073741824,
    )
    received = [across(terms[d], 2 * d) for d in order if d]
    groups = lax.axis_size("dp")
    rounds = groups.bit_length() - 1
    sums = {"value": value, "qk": qk}
    for step in range(rounds - 1):
        for name in sums:
            own = sums[name]
            sums[name] = local_call(add_kernel, block(head, BF16), (own, across_data(own, step), terms[0]), "add", 1048576)
    last = {name: across_data(sums[name], rounds - 1) for name in sums}
    token = local_call(sum_kernel, block(part, BF16), (terms[0], *received), "token_sum", 17179869184)
    q_mean, k_mean, v_mean = local_call(
        functools.partial(mean_kernel, groups),
        (block(half, F32), block(half, F32), jax.ShapeDtypeStruct((features, head), F32)),
        (sums["qk"], last["qk"], sums["value"], last["value"]), "weight_mean", 1048576,
    )
    return token[None], q_mean.T, k_mean.T, v_mean


def solution(mesh):
    rows = P("dp", "head", None)
    cols = P(None, "head")
    return jax.shard_map(
        body,
        mesh=mesh,
        in_specs=(rows, rows, cols, cols, cols, cols, cols, P("head"), P("head")),
        out_specs=(rows, cols, cols, cols),
        check_vma=False,
    )
```

```python
import functools

import jax
import jax.numpy as jnp
from jax import lax
from jax.experimental import pallas as pl
from jax.experimental.pallas import tpu as pltpu
from jax.sharding import PartitionSpec as P

CHUNK = 128
GROUP = 4
NORM_EPS = 1e-06
F32 = jnp.float32
BF16 = jnp.bfloat16


def nn(a, b):
    return lax.dot_general(a, b, (((1,), (0,)), ((), ())), preferred_element_type=F32)


def nt(a, b):
    return lax.dot_general(a, b, (((1,), (1,)), ((), ())), preferred_element_type=F32)


def tn(a, b):
    return lax.dot_general(a, b, (((0,), (0,)), ((), ())), preferred_element_type=F32)


def halves(a):
    high = a.astype(BF16)
    return high, (a - high.astype(F32)).astype(BF16)


def fine_nn(a, b):
    left = jnp.concatenate(a, 1)
    right = jnp.concatenate(b, 1)
    both = nn(left, jnp.concatenate([right, right], 0))
    width = b[0].shape[1]
    return both[:, :width] + both[:, width:]


def fine_gram(a):
    left = jnp.concatenate(a, 1)
    both = nt(left, jnp.concatenate([jnp.concatenate([p, p], 1) for p in a], 0))
    width = a[0].shape[0]
    return both[:, :width] + both[:, width:]


def row_sum(a):
    return jnp.sum(a, axis=1, keepdims=True)


def core_kernel(
    order,
    *refs,
):
    inputs, refs = refs[: 2 * len(order)], refs[2 * len(order) :]
    (
        narrow_ref, narrow2_ref, wv_ref, log_ref, bias_ref,
        rows_ref, near_ref, away_ref, vsum_ref, mine_ref, theirs_ref,
        cot_ref, value_ref, kk_s, qk_s, q_s, k_s, b_s, e_s, tail_s, gam_s, p_s, t_s, w_s, u0_s, kt_s, x_s, qn_s, kn_s,
        f_s, g_s, h_s, ec_s, m_s, d_s,
    ) = refs
    place = lax.axis_index("head")
    core, chip = lax.rem(place, 2), place // 2
    part = inputs[0].shape[0]
    features, head = rows_ref.shape[1], cot_ref.shape[1]
    column = pl.ds(pl.multiple_of(features + core * head, head), head)
    for slot, far in enumerate(order):
        for other in range(2):
            who = 2 * (chip ^ far) + (core ^ other)
            span = pl.ds(pl.multiple_of(who * part, part), part)
            message = inputs[2 * slot + other]
            rows_ref[span, :] = message[:, :features]
            cot_ref[span, :] = message[:, column]
    total = cot_ref.shape[0]
    num = total // CHUNK
    group = min(GROUP, num)
    scale = head ** -0.5
    row_id = lax.broadcasted_iota(jnp.int32, (CHUNK, CHUNK), 0)
    col_id = lax.broadcasted_iota(jnp.int32, (CHUNK, CHUNK), 1)
    low = row_id >= col_id
    strict = row_id > col_id
    low_ones = jnp.where(low, 1.0, 0.0).astype(BF16)
    high_ones = jnp.where(row_id <= col_id, 1.0, 0.0).astype(BF16)
    below_ones = jnp.where(strict, 1.0, 0.0).astype(BF16)
    rate = -jnp.exp(log_ref[...])
    bias = bias_ref[...]

    def loop(body):
        if num == group:
            body(0)
        else:
            lax.fori_loop(0, num // group, lambda i, c: (body(i * group), c)[1], 0)

    def at(first, i):
        if isinstance(first, int):
            return pl.ds((first + i) * CHUNK, CHUNK)
        return pl.ds(pl.multiple_of((first + i) * CHUNK, CHUNK), CHUNK)

    half = head // 2
    own, partner = narrow_ref, narrow2_ref
    spread = lambda row: jnp.broadcast_to(own[pl.ds(head, 16), :][row : row + 1], (head, features))
    narrow = jnp.concatenate(
        [own[:half, :], partner[:half, :], own[half:head, :], partner[half:head, :], spread(0), spread(1)], 0)

    def rows_of(first):
        if isinstance(first, int):
            return pl.ds(first * CHUNK, group * CHUNK)
        return pl.ds(pl.multiple_of(first * CHUNK, CHUNK), group * CHUNK)

    each = range(group)
    cut = lambda a: [a[i * CHUNK : (i + 1) * CHUNK] for i in each]
    join = lambda parts: jnp.concatenate(parts, 0)

    def prepare(first):
        here = rows_of(first)
        spans = [at(first, i) for i in each]
        rows = rows_ref[here, :]
        pre = nt(rows, narrow)
        v = nn(rows, wv_ref[...])
        qp, kp = pre[:, :head], pre[:, head : 2 * head]
        qn = lax.rsqrt(row_sum(qp * qp) + NORM_EPS) * scale
        kn = lax.rsqrt(row_sum(kp * kp) + NORM_EPS)
        q = qp * qn
        k = kp * kn
        beta = 1.0 / (1.0 + jnp.exp(-pre[:, 2 * head : 3 * head]))
        x = pre[:, 3 * head :] + bias
        g = rate * (jnp.maximum(x, 0.0) + jnp.log1p(jnp.exp(-jnp.abs(x))))
        g1 = g.astype(BF16)
        g2, g3 = halves(g - g1.astype(F32))
        split = cut(jnp.concatenate([g1, g2, g3], 1))
        sums = [nn(low_ones, split[i]) for i in each]
        cs = [s[:, :head] + (s[:, head : 2 * head] + s[:, 2 * head :]) for s in sums]
        lasts = [c[CHUNK - 1 : CHUNK, :] for c in cs]
        e = jnp.exp(join(cs))
        tail = jnp.exp(join([last - c for last, c in zip(lasts, cs)]))
        gam = jnp.exp(join([jnp.where(low, c - c.T, -1e30) for c in cs]))
        kpair = halves(k)
        khigh, klow = cut(kpair[0]), cut(kpair[1])
        q16 = cut(q.astype(BF16))
        kk = join([fine_gram((khigh[i], klow[i])) for i in each])
        qk = join([nt(q16[i], khigh[i]) for i in each])
        strict_all, low_all = join([strict] * group), join([low] * group)
        mats = cut(jnp.where(strict_all, beta * gam * kk, 0.0))
        p_all = (gam * qk).astype(BF16)
        kt_all = (tail * k).astype(BF16)
        ek_bv = cut(jnp.concatenate([beta * e * k, beta * v], 1))
        p, kt, eq = cut(p_all), cut(kt_all), cut(e * q)
        for ref, value in (
            (kk_s, kk), (qk_s, qk), (q_s, q), (k_s, k), (b_s, beta), (e_s, e), (tail_s, tail), (gam_s, gam), (x_s, x),
            (p_s, p_all), (kt_s, kt_all),
            (qn_s, jnp.broadcast_to(qn, q.shape)), (kn_s, jnp.broadcast_to(kn, q.shape)),
        ):
            ref[here, :] = value
        for i in each:
            ec_s[first + i] = jnp.exp(jnp.broadcast_to(lasts[i], (8, head)))
        eye = jnp.where(row_id == col_id, 1.0, 0.0)
        inv = [eye - jnp.where((row_id >> 1) == (col_id >> 1), a, 0.0) for a in mats]
        pairs = [halves(a) for a in mats]
        level = 1
        while (2 << level) <= CHUNK:
            joint = ((row_id >> (level + 1)) == (col_id >> (level + 1))) & ((row_id >> level) > (col_id >> level))
            tp = [halves(t) for t in inv]
            left = [
                fine_nn(tp[i], tuple(jnp.where(joint, half, jnp.zeros_like(half)) for half in pairs[i]))
                for i in each
            ]
            lp = [halves(z) for z in left]
            inv = [inv[i] - fine_nn(lp[i], tp[i]) for i in each]
            level += 1
        tp = [halves(t) for t in inv]
        ep = [halves(y) for y in ek_bv]
        wu = [
            nn(jnp.concatenate(tp[i], 1), jnp.concatenate([ep[i][0], ep[i][0]], 0)) + nn(tp[i][0], ep[i][1])
            for i in each
        ]
        w = [y[:, :head].astype(BF16) for y in wu]
        fg = [tn(kt[i], jnp.concatenate([w[i], wu[i][:, head:].astype(BF16)], 1)) for i in each]
        pw = [nn(p[i], w[i]) for i in each]
        hs = [tn((eq[i] - pw[i]).astype(BF16), cot_ref[spans[i], :]) for i in each]
        t_s[here, :] = join([t[0] for t in tp])
        w_s[here, :] = join(w)
        u0_s[here, :] = join([y[:, head:] for y in wu])
        f_s[here, :] = join([y[:, :head].astype(BF16) for y in fg])
        g_s[here, :] = join([y[:, head:] for y in fg])
        h_s[here, :] = join(hs)

    loop(prepare)

    m_s[pl.ds(0, head), :] = jnp.zeros((head, head), F32)
    d_s[pl.ds((num - 1) * head, head), :] = jnp.zeros((head, head), F32)
    m = jnp.zeros((head, head), F32)
    d = jnp.zeros((head, head), F32)
    for i in range(num):
        span = pl.ds(i * CHUNK, CHUNK)
        if i == 0:
            m = g_s[span, :]
        else:
            m = ec_s[i][:1] * m - nn(f_s[span, :], m.astype(BF16)) + g_s[span, :]
        m_s[pl.ds((i + 1) * head, head), :] = m
        r = num - 1 - i
        if r > 0:
            back = pl.ds(r * CHUNK, CHUNK)
            if r == num - 1:
                d = h_s[back, :]
            else:
                d = ec_s[r][:1] * d - tn(f_s[back, :], d.astype(BF16)) + h_s[back, :]
            d_s[pl.ds((r - 1) * head, head), :] = d

    def finish(first):
        here = rows_of(first)
        q, k, beta = q_s[here, :], k_s[here, :], b_s[here, :]
        gam, e, tail = gam_s[here, :], e_s[here, :], tail_s[here, :]
        do = cot_ref[here, :]
        m32, d32 = m_s[here, :], d_s[here, :]
        m, d = cut(m32.astype(BF16)), cut(d32.astype(BF16))
        q16, k16 = q.astype(BF16), k.astype(BF16)
        k_parts, qk_parts = cut(k16), [join([a, b]) for a, b in zip(cut(q16), cut(-k16))]
        p, kt, t, w, dos = cut(p_s[here, :]), cut(kt_s[here, :]), cut(t_s[here, :]), cut(w_s[here, :]), cut(do)
        strict_all = join([strict] * group)
        du = [tn(p[i], dos[i]) + nn(kt[i], d[i]) for i in each]
        u = u0_s[here, :] - join([nn(w[i], m[i]) for i in each])
        u16 = cut(u.astype(BF16))
        dr = join([tn(t[i], du[i].astype(BF16)) for i in each])
        dv = beta * dr
        dv16 = dv.astype(BF16)
        dvs = cut(dv16)
        wide = [nt(join([dos[i], dvs[i]]), join([u16[i], m[i]])) for i in each]
        ud = join([nt(u16[i], d[i]) for i in each])
        y32 = join([a[:CHUNK, :CHUNK] for a in wide]) * gam
        x32 = jnp.where(strict_all, join([a[CHUNK:, :CHUNK] for a in wide]) * gam, 0.0)
        yx = [join([a, b]) for a, b in zip(cut(y32.astype(BF16)), cut(x32.astype(BF16)))]
        by_k = [nn(yx[i], k_parts[i]) for i in each]
        by_qk = join([tn(yx[i], qk_parts[i]) for i in each])
        from_q = e * join([a[:CHUNK, CHUNK:] for a in wide])
        from_k = e * join([a[CHUNK:, CHUNK:] for a in wide])
        to_k = tail * ud
        dq = from_q + join([a[:CHUNK] for a in by_k])
        dk = to_k - from_k - join([a[CHUNK:] for a in by_k]) + by_qk
        zc = halves(jnp.where(strict_all, y32 * qk_s[here, :], 0.0) - x32 * kk_s[here, :])
        zr = halves(q * from_q - k * from_k)
        zt = cut(jnp.concatenate(halves(k * to_k), 1))
        zs = cut(jnp.concatenate([*zc, *zr], 1))
        up = join([nn(high_ones, zs[i]) for i in each])
        down = join([nn(below_ones, zt[i]) for i in each])
        crossing = jnp.where(strict_all, up[:, :head] + up[:, head : 2 * head], 0.0)
        single = up[:, 2 * head : 3 * head] + up[:, 3 * head :] + down[:, :head] + down[:, head:]
        carried = join([
            jnp.broadcast_to(row_sum(jnp.sum(ec_s[first + i][:1] * a, axis=0, keepdims=True)), (CHUNK, 1))
            for i, a in enumerate(cut(m32 * d32))
        ])
        dg = row_sum(crossing + single) + carried
        ga = (dg * rate) * (1.0 / (1.0 + jnp.exp(-x_s[here, :])))
        gb = row_sum(dr * u) * (1.0 - beta)
        gq = (qn_s[here, :] * (dq - q * (row_sum(q * dq) * head))).astype(BF16)
        gk = (kn_s[here, :] * (dk - k * row_sum(k * dk))).astype(BF16)
        lane = lax.broadcasted_iota(jnp.int32, q.shape, 1)
        gba = jnp.where(lane == 0, gb, jnp.where(lane == 1, ga, 0.0)).astype(BF16)
        near_ref[here, :] = jnp.concatenate([gq[:, :half], gk[:, :half]], 1)
        away_ref[here, :] = jnp.concatenate([gq[:, half:], gk[:, half:]], 1)
        value_ref[here, :] = dv16
        forth = jnp.concatenate([gq, gk, dv16, gba], 1)
        swapped = jnp.concatenate([gq[:, half:], gq[:, :half], gk[:, half:], gk[:, :half], dv16, gba], 1)
        first_core = core == 0
        pieces = group * CHUNK // (2 * part)
        for j in range(pieces):
            lo = slice(2 * j * part, (2 * j + 1) * part)
            hi = slice((2 * j + 1) * part, (2 * j + 2) * part)
            slot = first * CHUNK // (2 * part) + j
            to = pl.ds(slot * part if isinstance(slot, int) else pl.multiple_of(slot * part, part), part)
            mine_ref[to, :] = jnp.where(first_core, forth[lo], forth[hi])
            theirs_ref[to, :] = jnp.where(first_core, swapped[hi], swapped[lo])

    loop(finish)
    vsum_ref[...] = tn(value_ref[...], rows_ref[...]).astype(BF16)


def core_grads(order, messages, narrow, narrow2, wv, log_rate, rate_bias):
    part, features = messages[0].shape[0], wv.shape[0]
    head = wv.shape[1]
    total = part * len(messages)
    num = total // CHUNK
    col = lambda dt: pltpu.VMEM((total, head), dt)
    states = pltpu.VMEM(((num + 1) * head, head), F32)
    out = lambda rows, cols: jax.ShapeDtypeStruct((rows, cols), BF16)
    args = (*messages, narrow, narrow2, wv, log_rate, rate_bias)
    return pl.pallas_call(
        functools.partial(core_kernel, order),
        out_shape=(
            out(total, features), out(total, head), out(total, head), out(head, features),
            out(total // 2, 4 * head), out(total // 2, 4 * head),
        ),
        in_specs=[pl.BlockSpec(memory_space=pltpu.VMEM)] * len(args),
        out_specs=[pl.BlockSpec(memory_space=pltpu.VMEM)] * 6,
        scratch_shapes=[
            col(BF16), col(BF16), col(F32), col(F32),
            col(F32), col(F32), col(F32), col(F32), col(F32), col(F32), col(BF16), col(BF16), col(BF16), col(F32),
            col(BF16), col(F32), col(F32), col(F32),
            col(BF16), col(F32), col(F32), pltpu.VMEM((num, 8, head), F32), states, states,
        ],
        compiler_params=pltpu.CompilerParams(vmem_limit_bytes=48 * 1024 * 1024),
        name="core_grads",
    )(*args)


def pack_kernel(chips, hidden_ref, cot_ref, *outs):
    chip = lax.axis_index("head") // 2
    width, features = cot_ref.shape[1] // chips, hidden_ref.shape[1]
    for far, out in enumerate(outs):
        out[:, :features] = hidden_ref[...]
        out[:, features:] = cot_ref[:, pl.ds(pl.multiple_of((chip ^ far) * width, width), width)]


def narrow_kernel(wq_ref, wk_ref, wb_ref, wa_ref, after_ref, out_ref):
    half, features = wq_ref.shape
    out_ref[pl.ds(0, half), :] = wq_ref[...]
    out_ref[pl.ds(half, half), :] = wk_ref[...]
    line = lax.broadcasted_iota(jnp.int32, (16, features), 0)
    beta, decay = wb_ref[...].astype(F32), wa_ref[...].astype(F32)
    out_ref[pl.ds(2 * half, 16), :] = jnp.where(line == 0, beta, jnp.where(line == 1, decay, 0.0)).astype(BF16)


def gram_kernel(rows_ref, near_ref, away_ref, out_ref):
    rows = rows_ref[...]
    out_ref[...] = (tn(near_ref[...], rows) + tn(away_ref[...], rows)).astype(BF16)


def term_kernel(part, mine_ref, recv_ref, own, partner, wv_ref, wv2_ref, *outs):
    outs, all_ref = outs[:-1], outs[-1]
    chip = lax.axis_index("head") // 2
    head = wv_ref.shape[1]
    half = head // 2
    narrow = jnp.concatenate([own[:half, :], partner[:half, :], own[half:head, :], partner[half:head, :]], 0)
    small, small2 = own[pl.ds(head, 16), :], partner[pl.ds(head, 16), :]
    mine, recv = mine_ref[...], recv_ref[...]
    both = nn(jnp.concatenate([mine[:, : 2 * head], recv[:, : 2 * head]], 1), jnp.concatenate([narrow, narrow], 0))
    both = both + nt(
        jnp.concatenate([mine[:, 2 * head : 3 * head], recv[:, 2 * head : 3 * head]], 1),
        jnp.concatenate([wv_ref[...], wv2_ref[...]], 1))
    both = both + nn(mine[:, 3 * head : 3 * head + 16], small) + nn(recv[:, 3 * head : 3 * head + 16], small2)
    all_ref[...] = both.astype(BF16)
    for far, out in enumerate(outs):
        out[...] = all_ref[pl.ds(pl.multiple_of((chip ^ far) * part, part), part), :]


def sum_kernel(count, *refs):
    total = refs[0][...].astype(F32)
    for ref in refs[1:count]:
        total = total + ref[...].astype(F32)
    refs[-1][...] = total.astype(BF16)


def mean_kernel(count, own_qk, recv_qk, own_v, recv_v, q_ref, k_ref, v_ref):
    half = q_ref.shape[0]
    qk = (own_qk[...].astype(F32) + recv_qk[...].astype(F32)) * (1.0 / count)
    q_ref[...] = qk[:half]
    k_ref[...] = qk[half:]
    v_ref[...] = ((own_v[...].astype(F32) + recv_v[...].astype(F32)) * (1.0 / count)).T


def add_kernel(own_ref, recv_ref, after_ref, out_ref):
    out_ref[...] = (own_ref[...].astype(F32) + recv_ref[...].astype(F32)).astype(BF16)


def local_call(body, outs, args, name, flops, scratch=(), after=()):
    many = isinstance(outs, tuple)
    spec = pl.BlockSpec(memory_space=pltpu.VMEM)
    return pl.pallas_call(
        body,
        out_shape=outs,
        in_specs=[spec] * len(args) + [pl.BlockSpec(memory_space=pl.ANY)] * len(after),
        out_specs=[spec] * len(outs) if many else spec,
        scratch_shapes=scratch,
        compiler_params=pltpu.CompilerParams(vmem_limit_bytes=48 * 1024 * 1024),
        cost_estimate=pl.CostEstimate(flops=flops, bytes_accessed=1 << 20, transcendentals=0),
        name=name,
    )(*args, *after)


def across(block, distance):
    count = lax.axis_size("head")
    return lax.ppermute(block, "head", [(i, i ^ distance) for i in range(count)])


def across_data(block, step):
    groups, places = lax.axis_size("dp"), lax.axis_size("head")
    bits = groups.bit_length() - 1
    route = []
    for g in range(groups):
        for p in range(places):
            bit = step if p % 2 == 0 else bits - 1 - step
            route.append((g * places + p, (g ^ (1 << bit)) * places + p))
    return lax.ppermute(block, ("dp", "head"), route)


def body(
    hidden, core_grad, query_weight, key_weight, value_weight, beta_weight, decay_weight, decay_log, decay_bias,
):
    half = query_weight.shape[1]
    head = value_weight.shape[1]
    chips = lax.axis_size("head") // 2
    part, features = hidden.shape[1:]
    order = sorted(range(chips), key=lambda d: -d)
    block = lambda rows, dt: jax.ShapeDtypeStruct((rows, features), dt)
    message = jax.ShapeDtypeStruct((part, features + 2 * head), BF16)
    sent = local_call(
        functools.partial(pack_kernel, chips), (message,) * chips, (hidden[0], core_grad[0]), "pack", 1048576)
    got = {d: across(sent[d], 2 * d) if d else sent[0] for d in order}
    narrow = local_call(
        narrow_kernel, block(head + 16, BF16),
        (query_weight.T, key_weight.T, beta_weight.T, decay_weight.T, got[order[0]]), "narrow", 1048576)
    messages = []
    for d in order:
        messages += [got[d], across(got[d], 1)]
    narrow2, wv2 = across(narrow, 1), across(value_weight, 1)

    all_rows, near, away, value, mine, theirs = core_grads(
        order, messages, narrow, narrow2, value_weight, decay_log.reshape(1, 1), decay_bias.reshape(1, 1))
    recv = across(away, 1)
    other = across(theirs, 1)
    qk = local_call(gram_kernel, block(head, BF16), (all_rows, near, recv), "gram", 268435456)
    terms = local_call(
        functools.partial(term_kernel, part), (block(part, BF16),) * chips,
        (mine, other, narrow, narrow2, value_weight, wv2), "terms", 1073741824,
        [pltpu.VMEM((mine.shape[0], features), BF16)],
    )
    received = [across(terms[d], 2 * d) for d in order if d]
    groups = lax.axis_size("dp")
    rounds = groups.bit_length() - 1
    sums = {"value": value, "qk": qk}
    for step in range(rounds - 1):
        for name in sums:
            own = sums[name]
            sums[name] = local_call(add_kernel, block(head, BF16), (own, across_data(own, step), terms[0]), "add", 1048576)
    last = {name: across_data(sums[name], rounds - 1) for name in sums}
    q_mean, k_mean, v_mean = local_call(
        functools.partial(mean_kernel, groups),
        (block(half, F32), block(half, F32), jax.ShapeDtypeStruct((features, head), F32)),
        (sums["qk"], last["qk"], sums["value"], last["value"]), "mean", 1048576)
    token = local_call(
        functools.partial(sum_kernel, chips), block(part, BF16), (terms[0], *received), "token_sum", 17179869184, after=())
    return token[None], q_mean.T, k_mean.T, v_mean


def solution(mesh):
    rows = P("dp", "head", None)
    cols = P(None, "head")
    return jax.shard_map(
        body,
        mesh=mesh,
        in_specs=(rows, rows, cols, cols, cols, cols, cols, P("head"), P("head")),
        out_specs=(rows, cols, cols, cols),
        check_vma=False,
    )
```

```python
import functools

import jax
import jax.numpy as jnp
from jax import lax
from jax.experimental import pallas as pl
from jax.experimental.pallas import tpu as pltpu
from jax.sharding import PartitionSpec as P

CHUNK = 128
GROUP = 4
NORM_EPS = 1e-06
F32 = jnp.float32
BF16 = jnp.bfloat16


def nn(a, b):
    return lax.dot_general(a, b, (((1,), (0,)), ((), ())), preferred_element_type=F32)


def nt(a, b):
    return lax.dot_general(a, b, (((1,), (1,)), ((), ())), preferred_element_type=F32)


def tn(a, b):
    return lax.dot_general(a, b, (((0,), (0,)), ((), ())), preferred_element_type=F32)


def halves(a):
    high = a.astype(BF16)
    return high, (a - high.astype(F32)).astype(BF16)


def fine_nn(a, b):
    left = jnp.concatenate(a, 1)
    right = jnp.concatenate(b, 1)
    both = nn(left, jnp.concatenate([right, right], 0))
    width = b[0].shape[1]
    return both[:, :width] + both[:, width:]


def fine_gram(a):
    left = jnp.concatenate(a, 1)
    both = nt(left, jnp.concatenate([jnp.concatenate([p, p], 1) for p in a], 0))
    width = a[0].shape[0]
    return both[:, :width] + both[:, width:]


def row_sum(a):
    return jnp.sum(a, axis=1, keepdims=True)


def core_kernel(
    order,
    *refs,
):
    inputs, refs = refs[: 2 * len(order)], refs[2 * len(order) :]
    (
        narrow_ref, narrow2_ref, wv_ref, log_ref, bias_ref,
        rows_ref, near_ref, away_ref, vsum_ref, mine_ref, theirs_ref,
        cot_ref, value_ref, kk_s, qk_s, q_s, k_s, b_s, e_s, tail_s, gam_s, p_s, t_s, w_s, u0_s, kt_s, x_s, qn_s, kn_s,
        f_s, g_s, h_s, ec_s, m_s, d_s,
    ) = refs
    place = lax.axis_index("head")
    core, chip = lax.rem(place, 2), place // 2
    part = inputs[0].shape[0]
    features, head = rows_ref.shape[1], cot_ref.shape[1]
    column = pl.ds(pl.multiple_of(features + core * head, head), head)
    for slot, far in enumerate(order):
        for other in range(2):
            who = 2 * (chip ^ far) + (core ^ other)
            span = pl.ds(pl.multiple_of(who * part, part), part)
            message = inputs[2 * slot + other]
            rows_ref[span, :] = message[:, :features]
            cot_ref[span, :] = message[:, column]
    total = cot_ref.shape[0]
    num = total // CHUNK
    group = min(GROUP, num)
    scale = head ** -0.5
    row_id = lax.broadcasted_iota(jnp.int32, (CHUNK, CHUNK), 0)
    col_id = lax.broadcasted_iota(jnp.int32, (CHUNK, CHUNK), 1)
    low = row_id >= col_id
    strict = row_id > col_id
    low_ones = jnp.where(low, 1.0, 0.0).astype(BF16)
    high_ones = jnp.where(row_id <= col_id, 1.0, 0.0).astype(BF16)
    below_ones = jnp.where(strict, 1.0, 0.0).astype(BF16)
    rate = -jnp.exp(log_ref[...])
    bias = bias_ref[...]

    def loop(body):
        if num == group:
            body(0)
        else:
            lax.fori_loop(0, num // group, lambda i, c: (body(i * group), c)[1], 0)

    def at(first, i):
        if isinstance(first, int):
            return pl.ds((first + i) * CHUNK, CHUNK)
        return pl.ds(pl.multiple_of((first + i) * CHUNK, CHUNK), CHUNK)

    half = head // 2
    own, partner = narrow_ref, narrow2_ref
    spread = lambda row: jnp.broadcast_to(own[pl.ds(head, 16), :][row : row + 1], (head, features))
    narrow = jnp.concatenate(
        [own[:half, :], partner[:half, :], own[half:head, :], partner[half:head, :], spread(0), spread(1)], 0)

    def rows_of(first):
        if isinstance(first, int):
            return pl.ds(first * CHUNK, group * CHUNK)
        return pl.ds(pl.multiple_of(first * CHUNK, CHUNK), group * CHUNK)

    each = range(group)
    cut = lambda a: [a[i * CHUNK : (i + 1) * CHUNK] for i in each]
    join = lambda parts: jnp.concatenate(parts, 0)

    def prepare(first):
        here = rows_of(first)
        spans = [at(first, i) for i in each]
        rows = rows_ref[here, :]
        pre = nt(rows, narrow)
        v = nn(rows, wv_ref[...])
        qp, kp = pre[:, :head], pre[:, head : 2 * head]
        qn = lax.rsqrt(row_sum(qp * qp) + NORM_EPS) * scale
        kn = lax.rsqrt(row_sum(kp * kp) + NORM_EPS)
        q = qp * qn
        k = kp * kn
        beta = 1.0 / (1.0 + jnp.exp(-pre[:, 2 * head : 3 * head]))
        x = pre[:, 3 * head :] + bias
        g = rate * (jnp.maximum(x, 0.0) + jnp.log1p(jnp.exp(-jnp.abs(x))))
        g1 = g.astype(BF16)
        g2, g3 = halves(g - g1.astype(F32))
        split = cut(jnp.concatenate([g1, g2, g3], 1))
        sums = [nn(low_ones, split[i]) for i in each]
        cs = [s[:, :head] + (s[:, head : 2 * head] + s[:, 2 * head :]) for s in sums]
        lasts = [c[CHUNK - 1 : CHUNK, :] for c in cs]
        e = jnp.exp(join(cs))
        tail = jnp.exp(join([last - c for last, c in zip(lasts, cs)]))
        gam = jnp.exp(join([jnp.where(low, c - c.T, -1e30) for c in cs]))
        kpair = halves(k)
        khigh, klow = cut(kpair[0]), cut(kpair[1])
        q16 = cut(q.astype(BF16))
        kk = join([fine_gram((khigh[i], klow[i])) for i in each])
        qk = join([nt(q16[i], khigh[i]) for i in each])
        strict_all, low_all = join([strict] * group), join([low] * group)
        mats = cut(jnp.where(strict_all, beta * gam * kk, 0.0))
        p_all = (gam * qk).astype(BF16)
        kt_all = (tail * k).astype(BF16)
        ek_bv = cut(jnp.concatenate([beta * e * k, beta * v], 1))
        p, kt, eq = cut(p_all), cut(kt_all), cut(e * q)
        for ref, value in (
            (kk_s, kk), (qk_s, qk), (q_s, q), (k_s, k), (b_s, beta), (e_s, e), (tail_s, tail), (gam_s, gam), (x_s, x),
            (p_s, p_all), (kt_s, kt_all),
            (qn_s, jnp.broadcast_to(qn, q.shape)), (kn_s, jnp.broadcast_to(kn, q.shape)),
        ):
            ref[here, :] = value
        for i in each:
            ec_s[first + i] = jnp.exp(jnp.broadcast_to(lasts[i], (8, head)))
        eye = jnp.where(row_id == col_id, 1.0, 0.0)
        inv = [eye - jnp.where((row_id >> 1) == (col_id >> 1), a, 0.0) for a in mats]
        pairs = [halves(a) for a in mats]
        level = 1
        while (2 << level) <= CHUNK:
            joint = ((row_id >> (level + 1)) == (col_id >> (level + 1))) & ((row_id >> level) > (col_id >> level))
            tp = [halves(t) for t in inv]
            left = [
                fine_nn(tp[i], tuple(jnp.where(joint, half, jnp.zeros_like(half)) for half in pairs[i]))
                for i in each
            ]
            lp = [halves(z) for z in left]
            inv = [inv[i] - fine_nn(lp[i], tp[i]) for i in each]
            level += 1
        tp = [halves(t) for t in inv]
        ep = [halves(y) for y in ek_bv]
        wu = [
            nn(jnp.concatenate(tp[i], 1), jnp.concatenate([ep[i][0], ep[i][0]], 0)) + nn(tp[i][0], ep[i][1])
            for i in each
        ]
        w = [y[:, :head].astype(BF16) for y in wu]
        fg = [tn(kt[i], jnp.concatenate([w[i], wu[i][:, head:].astype(BF16)], 1)) for i in each]
        pw = [nn(p[i], w[i]) for i in each]
        hs = [tn((eq[i] - pw[i]).astype(BF16), cot_ref[spans[i], :]) for i in each]
        t_s[here, :] = join([t[0] for t in tp])
        w_s[here, :] = join(w)
        u0_s[here, :] = join([y[:, head:] for y in wu])
        f_s[here, :] = join([y[:, :head].astype(BF16) for y in fg])
        g_s[here, :] = join([y[:, head:] for y in fg])
        h_s[here, :] = join(hs)

    loop(prepare)

    m_s[pl.ds(0, head), :] = jnp.zeros((head, head), F32)
    d_s[pl.ds((num - 1) * head, head), :] = jnp.zeros((head, head), F32)
    m = jnp.zeros((head, head), F32)
    d = jnp.zeros((head, head), F32)
    for i in range(num):
        span = pl.ds(i * CHUNK, CHUNK)
        if i == 0:
            m = g_s[span, :]
        else:
            m = ec_s[i][:1] * m - nn(f_s[span, :], m.astype(BF16)) + g_s[span, :]
        m_s[pl.ds((i + 1) * head, head), :] = m
        r = num - 1 - i
        if r > 0:
            back = pl.ds(r * CHUNK, CHUNK)
            if r == num - 1:
                d = h_s[back, :]
            else:
                d = ec_s[r][:1] * d - tn(f_s[back, :], d.astype(BF16)) + h_s[back, :]
            d_s[pl.ds((r - 1) * head, head), :] = d

    def finish(first):
        here = rows_of(first)
        q, k, beta = q_s[here, :], k_s[here, :], b_s[here, :]
        gam, e, tail = gam_s[here, :], e_s[here, :], tail_s[here, :]
        do = cot_ref[here, :]
        m32, d32 = m_s[here, :], d_s[here, :]
        m, d = cut(m32.astype(BF16)), cut(d32.astype(BF16))
        q16, k16 = q.astype(BF16), k.astype(BF16)
        k_parts, qk_parts = cut(k16), [join([a, b]) for a, b in zip(cut(q16), cut(-k16))]
        p, kt, t, w, dos = cut(p_s[here, :]), cut(kt_s[here, :]), cut(t_s[here, :]), cut(w_s[here, :]), cut(do)
        strict_all = join([strict] * group)
        du = [tn(p[i], dos[i]) + nn(kt[i], d[i]) for i in each]
        u = u0_s[here, :] - join([nn(w[i], m[i]) for i in each])
        u16 = cut(u.astype(BF16))
        dr = join([tn(t[i], du[i].astype(BF16)) for i in each])
        dv = beta * dr
        dv16 = dv.astype(BF16)
        dvs = cut(dv16)
        wide = [nt(join([dos[i], dvs[i]]), join([u16[i], m[i]])) for i in each]
        ud = join([nt(u16[i], d[i]) for i in each])
        y32 = join([a[:CHUNK, :CHUNK] for a in wide]) * gam
        x32 = jnp.where(strict_all, join([a[CHUNK:, :CHUNK] for a in wide]) * gam, 0.0)
        yx = [join([a, b]) for a, b in zip(cut(y32.astype(BF16)), cut(x32.astype(BF16)))]
        by_k = [nn(yx[i], k_parts[i]) for i in each]
        by_qk = join([tn(yx[i], qk_parts[i]) for i in each])
        from_q = e * join([a[:CHUNK, CHUNK:] for a in wide])
        from_k = e * join([a[CHUNK:, CHUNK:] for a in wide])
        to_k = tail * ud
        dq = from_q + join([a[:CHUNK] for a in by_k])
        dk = to_k - from_k - join([a[CHUNK:] for a in by_k]) + by_qk
        zc = halves(jnp.where(strict_all, y32 * qk_s[here, :], 0.0) - x32 * kk_s[here, :])
        zr = halves(q * from_q - k * from_k)
        zt = cut(jnp.concatenate(halves(k * to_k), 1))
        zs = cut(jnp.concatenate([*zc, *zr], 1))
        up = join([nn(high_ones, zs[i]) for i in each])
        down = join([nn(below_ones, zt[i]) for i in each])
        crossing = jnp.where(strict_all, up[:, :head] + up[:, head : 2 * head], 0.0)
        single = up[:, 2 * head : 3 * head] + up[:, 3 * head :] + down[:, :head] + down[:, head:]
        carried = join([
            jnp.broadcast_to(row_sum(jnp.sum(ec_s[first + i][:1] * a, axis=0, keepdims=True)), (CHUNK, 1))
            for i, a in enumerate(cut(m32 * d32))
        ])
        dg = row_sum(crossing + single) + carried
        ga = (dg * rate) * (1.0 / (1.0 + jnp.exp(-x_s[here, :])))
        gb = row_sum(dr * u) * (1.0 - beta)
        gq = (qn_s[here, :] * (dq - q * (row_sum(q * dq) * head))).astype(BF16)
        gk = (kn_s[here, :] * (dk - k * row_sum(k * dk))).astype(BF16)
        lane = lax.broadcasted_iota(jnp.int32, q.shape, 1)
        gba = jnp.where(lane == 0, gb, jnp.where(lane == 1, ga, 0.0)).astype(BF16)
        near_ref[here, :] = jnp.concatenate([gq[:, :half], gk[:, :half]], 1)
        away_ref[here, :] = jnp.concatenate([gq[:, half:], gk[:, half:]], 1)
        value_ref[here, :] = dv16
        forth = jnp.concatenate([gq, gk, dv16, gba], 1)
        swapped = jnp.concatenate([gq[:, half:], gq[:, :half], gk[:, half:], gk[:, :half], dv16, gba], 1)
        first_core = core == 0
        pieces = group * CHUNK // (2 * part)
        for j in range(pieces):
            lo = slice(2 * j * part, (2 * j + 1) * part)
            hi = slice((2 * j + 1) * part, (2 * j + 2) * part)
            slot = first * CHUNK // (2 * part) + j
            to = pl.ds(slot * part if isinstance(slot, int) else pl.multiple_of(slot * part, part), part)
            mine_ref[to, :] = jnp.where(first_core, forth[lo], forth[hi])
            theirs_ref[to, :] = jnp.where(first_core, swapped[hi], swapped[lo])

    loop(finish)
    vsum_ref[...] = tn(value_ref[...], rows_ref[...]).astype(BF16)


def core_grads(order, messages, narrow, narrow2, wv, log_rate, rate_bias):
    part, features = messages[0].shape[0], wv.shape[0]
    head = wv.shape[1]
    total = part * len(messages)
    num = total // CHUNK
    col = lambda dt: pltpu.VMEM((total, head), dt)
    states = pltpu.VMEM(((num + 1) * head, head), F32)
    out = lambda rows, cols: jax.ShapeDtypeStruct((rows, cols), BF16)
    args = (*messages, narrow, narrow2, wv, log_rate, rate_bias)
    return pl.pallas_call(
        functools.partial(core_kernel, order),
        out_shape=(
            out(total, features), out(total, head), out(total, head), out(head, features),
            out(total // 2, 4 * head), out(total // 2, 4 * head),
        ),
        in_specs=[pl.BlockSpec(memory_space=pltpu.VMEM)] * len(args),
        out_specs=[pl.BlockSpec(memory_space=pltpu.VMEM)] * 6,
        scratch_shapes=[
            col(BF16), col(BF16), col(F32), col(F32),
            col(F32), col(F32), col(F32), col(F32), col(F32), col(F32), col(BF16), col(BF16), col(BF16), col(F32),
            col(BF16), col(F32), col(F32), col(F32),
            col(BF16), col(F32), col(F32), pltpu.VMEM((num, 8, head), F32), states, states,
        ],
        compiler_params=pltpu.CompilerParams(vmem_limit_bytes=48 * 1024 * 1024),
        name="core_grads",
    )(*args)


def pack_kernel(chips, hidden_ref, cot_ref, *outs):
    chip = lax.axis_index("head") // 2
    width, features = cot_ref.shape[1] // chips, hidden_ref.shape[1]
    for far, out in enumerate(outs):
        out[:, :features] = hidden_ref[...]
        out[:, features:] = cot_ref[:, pl.ds(pl.multiple_of((chip ^ far) * width, width), width)]


def narrow_kernel(wq_ref, wk_ref, wb_ref, wa_ref, after_ref, out_ref):
    half, features = wq_ref.shape
    out_ref[pl.ds(0, half), :] = wq_ref[...]
    out_ref[pl.ds(half, half), :] = wk_ref[...]
    line = lax.broadcasted_iota(jnp.int32, (16, features), 0)
    beta, decay = wb_ref[...].astype(F32), wa_ref[...].astype(F32)
    out_ref[pl.ds(2 * half, 16), :] = jnp.where(line == 0, beta, jnp.where(line == 1, decay, 0.0)).astype(BF16)


def gram_kernel(rows_ref, near_ref, away_ref, out_ref):
    rows = rows_ref[...]
    out_ref[...] = (tn(near_ref[...], rows) + tn(away_ref[...], rows)).astype(BF16)


def term_kernel(part, mine_ref, recv_ref, own, partner, wv_ref, wv2_ref, *outs):
    outs, all_ref = outs[:-1], outs[-1]
    chip = lax.axis_index("head") // 2
    head = wv_ref.shape[1]
    half = head // 2
    narrow = jnp.concatenate([own[:half, :], partner[:half, :], own[half:head, :], partner[half:head, :]], 0)
    small, small2 = own[pl.ds(head, 16), :], partner[pl.ds(head, 16), :]
    mine, recv = mine_ref[...], recv_ref[...]
    both = nn(jnp.concatenate([mine[:, : 2 * head], recv[:, : 2 * head]], 1), jnp.concatenate([narrow, narrow], 0))
    both = both + nt(
        jnp.concatenate([mine[:, 2 * head : 3 * head], recv[:, 2 * head : 3 * head]], 1),
        jnp.concatenate([wv_ref[...], wv2_ref[...]], 1))
    both = both + nn(mine[:, 3 * head : 3 * head + 16], small) + nn(recv[:, 3 * head : 3 * head + 16], small2)
    all_ref[...] = both.astype(BF16)
    for far, out in enumerate(outs):
        out[...] = all_ref[pl.ds(pl.multiple_of((chip ^ far) * part, part), part), :]


def sum_kernel(count, *refs):
    total = refs[0][...].astype(F32)
    for ref in refs[1:count]:
        total = total + ref[...].astype(F32)
    refs[-1][...] = total


def last_kernel(count, own_qk, recv_qk, own_v, recv_v, *refs):
    blocks, (q_ref, k_ref, v_ref, token_ref) = refs[:-4], refs[-4:]
    half = q_ref.shape[0]
    qk = (own_qk[...].astype(F32) + recv_qk[...].astype(F32)) * (1.0 / count)
    q_ref[...] = qk[:half]
    k_ref[...] = qk[half:]
    v_ref[...] = ((own_v[...].astype(F32) + recv_v[...].astype(F32)) * (1.0 / count)).T
    total = blocks[0][...].astype(F32)
    for ref in blocks[1:]:
        total = total + ref[...].astype(F32)
    token_ref[...] = total.astype(BF16)


def add_kernel(own_ref, recv_ref, after_ref, out_ref):
    out_ref[...] = (own_ref[...].astype(F32) + recv_ref[...].astype(F32)).astype(BF16)


def local_call(body, outs, args, name, flops, scratch=(), after=()):
    many = isinstance(outs, tuple)
    spec = pl.BlockSpec(memory_space=pltpu.VMEM)
    return pl.pallas_call(
        body,
        out_shape=outs,
        in_specs=[spec] * len(args) + [pl.BlockSpec(memory_space=pl.ANY)] * len(after),
        out_specs=[spec] * len(outs) if many else spec,
        scratch_shapes=scratch,
        compiler_params=pltpu.CompilerParams(vmem_limit_bytes=48 * 1024 * 1024),
        cost_estimate=pl.CostEstimate(flops=flops, bytes_accessed=1 << 20, transcendentals=0),
        name=name,
    )(*args, *after)


def across(block, distance):
    count = lax.axis_size("head")
    return lax.ppermute(block, "head", [(i, i ^ distance) for i in range(count)])


def across_data(block, step):
    groups, places = lax.axis_size("dp"), lax.axis_size("head")
    bits = groups.bit_length() - 1
    route = []
    for g in range(groups):
        for p in range(places):
            bit = step if p % 2 == 0 else bits - 1 - step
            route.append((g * places + p, (g ^ (1 << bit)) * places + p))
    return lax.ppermute(block, ("dp", "head"), route)


def body(
    hidden, core_grad, query_weight, key_weight, value_weight, beta_weight, decay_weight, decay_log, decay_bias,
):
    half = query_weight.shape[1]
    head = value_weight.shape[1]
    chips = lax.axis_size("head") // 2
    part, features = hidden.shape[1:]
    order = sorted(range(chips), key=lambda d: -d)
    block = lambda rows, dt: jax.ShapeDtypeStruct((rows, features), dt)
    message = jax.ShapeDtypeStruct((part, features + 2 * head), BF16)
    sent = local_call(
        functools.partial(pack_kernel, chips), (message,) * chips, (hidden[0], core_grad[0]), "pack", 1048576)
    got = {d: across(sent[d], 2 * d) if d else sent[0] for d in order}
    narrow = local_call(
        narrow_kernel, block(head + 16, BF16),
        (query_weight.T, key_weight.T, beta_weight.T, decay_weight.T, got[order[0]]), "narrow", 1048576)
    messages = []
    for d in order:
        messages += [got[d], across(got[d], 1)]
    narrow2, wv2 = across(narrow, 1), across(value_weight, 1)

    all_rows, near, away, value, mine, theirs = core_grads(
        order, messages, narrow, narrow2, value_weight, decay_log.reshape(1, 1), decay_bias.reshape(1, 1))
    recv = across(away, 1)
    other = across(theirs, 1)
    qk = local_call(gram_kernel, block(head, BF16), (all_rows, near, recv), "gram", 268435456)
    terms = local_call(
        functools.partial(term_kernel, part), (block(part, BF16),) * chips,
        (mine, other, narrow, narrow2, value_weight, wv2), "terms", 1073741824,
        [pltpu.VMEM((mine.shape[0], features), BF16)],
    )
    received = [across(terms[d], 2 * d) for d in order if d]
    groups = lax.axis_size("dp")
    rounds = groups.bit_length() - 1
    sums = {"value": value, "qk": qk}
    for step in range(rounds - 1):
        for name in sums:
            own = sums[name]
            sums[name] = local_call(add_kernel, block(head, BF16), (own, across_data(own, step), terms[0]), "add", 1048576)
    last = {name: across_data(sums[name], rounds - 1) for name in sums}
    begun = local_call(
        functools.partial(sum_kernel, 2), block(part, F32), (terms[0], received[0]), "token_begin", 17179869184)
    q_mean, k_mean, v_mean, token = local_call(
        functools.partial(last_kernel, groups),
        (block(half, F32), block(half, F32), jax.ShapeDtypeStruct((features, head), F32), block(part, BF16)),
        (sums["qk"], last["qk"], sums["value"], last["value"], begun, *received[1:]), "last", 1048576)
    return token[None], q_mean.T, k_mean.T, v_mean


def solution(mesh):
    rows = P("dp", "head", None)
    cols = P(None, "head")
    return jax.shard_map(
        body,
        mesh=mesh,
        in_specs=(rows, rows, cols, cols, cols, cols, cols, P("head"), P("head")),
        out_specs=(rows, cols, cols, cols),
        check_vma=False,
    )
```

```python
import functools

import jax
import jax.numpy as jnp
from jax import lax
from jax.experimental import pallas as pl
from jax.experimental.pallas import tpu as pltpu
from jax.sharding import PartitionSpec as P

CHUNK = 128
GROUP = 4
NORM_EPS = 1e-06
F32 = jnp.float32
BF16 = jnp.bfloat16


def nn(a, b):
    return lax.dot_general(a, b, (((1,), (0,)), ((), ())), preferred_element_type=F32)


def nt(a, b):
    return lax.dot_general(a, b, (((1,), (1,)), ((), ())), preferred_element_type=F32)


def tn(a, b):
    return lax.dot_general(a, b, (((0,), (0,)), ((), ())), preferred_element_type=F32)


def halves(a):
    high = a.astype(BF16)
    return high, (a - high.astype(F32)).astype(BF16)


def fine_nn(a, b):
    left = jnp.concatenate(a, 1)
    right = jnp.concatenate(b, 1)
    both = nn(left, jnp.concatenate([right, right], 0))
    width = b[0].shape[1]
    return both[:, :width] + both[:, width:]


def fine_gram(a):
    left = jnp.concatenate(a, 1)
    both = nt(left, jnp.concatenate([jnp.concatenate([p, p], 1) for p in a], 0))
    width = a[0].shape[0]
    return both[:, :width] + both[:, width:]


def row_sum(a):
    return jnp.sum(a, axis=1, keepdims=True)


def core_kernel(
    order,
    *refs,
):
    inputs, refs = refs[: 2 * len(order)], refs[2 * len(order) :]
    (
        narrow_ref, narrow2_ref, wv_ref, log_ref, bias_ref,
        rows_ref, near_ref, away_ref, vsum_ref, mine_ref, theirs_ref,
        cot_ref, value_ref, kk_s, qk_s, q_s, k_s, b_s, e_s, tail_s, gam_s, p_s, t_s, w_s, u0_s, kt_s, x_s, qn_s, kn_s,
        f_s, g_s, h_s, ec_s, m_s, d_s,
    ) = refs
    place = lax.axis_index("head")
    core, chip = lax.rem(place, 2), place // 2
    part = inputs[0].shape[0]
    features, head = rows_ref.shape[1], cot_ref.shape[1]
    column = pl.ds(pl.multiple_of(features + core * head, head), head)
    for slot, far in enumerate(order):
        for other in range(2):
            who = 2 * (chip ^ far) + (core ^ other)
            span = pl.ds(pl.multiple_of(who * part, part), part)
            message = inputs[2 * slot + other]
            rows_ref[span, :] = message[:, :features]
            cot_ref[span, :] = message[:, column]
    total = cot_ref.shape[0]
    num = total // CHUNK
    group = min(GROUP, num)
    scale = head ** -0.5
    row_id = lax.broadcasted_iota(jnp.int32, (CHUNK, CHUNK), 0)
    col_id = lax.broadcasted_iota(jnp.int32, (CHUNK, CHUNK), 1)
    low = row_id >= col_id
    strict = row_id > col_id
    low_ones = jnp.where(low, 1.0, 0.0).astype(BF16)
    high_ones = jnp.where(row_id <= col_id, 1.0, 0.0).astype(BF16)
    below_ones = jnp.where(strict, 1.0, 0.0).astype(BF16)
    rate = -jnp.exp(log_ref[...])
    bias = bias_ref[...]

    def loop(body):
        if num == group:
            body(0)
        else:
            lax.fori_loop(0, num // group, lambda i, c: (body(i * group), c)[1], 0)

    def at(first, i):
        if isinstance(first, int):
            return pl.ds((first + i) * CHUNK, CHUNK)
        return pl.ds(pl.multiple_of((first + i) * CHUNK, CHUNK), CHUNK)

    half = head // 2
    own, partner = narrow_ref, narrow2_ref
    spread = lambda row: jnp.broadcast_to(own[pl.ds(head, 16), :][row : row + 1], (head, features))
    narrow = jnp.concatenate(
        [own[:half, :], partner[:half, :], own[half:head, :], partner[half:head, :], spread(0), spread(1)], 0)

    def rows_of(first):
        if isinstance(first, int):
            return pl.ds(first * CHUNK, group * CHUNK)
        return pl.ds(pl.multiple_of(first * CHUNK, CHUNK), group * CHUNK)

    each = range(group)
    cut = lambda a: [a[i * CHUNK : (i + 1) * CHUNK] for i in each]
    join = lambda parts: jnp.concatenate(parts, 0)

    def prepare(first):
        here = rows_of(first)
        spans = [at(first, i) for i in each]
        rows = rows_ref[here, :]
        pre = nt(rows, narrow)
        v = nn(rows, wv_ref[...])
        qp, kp = pre[:, :head], pre[:, head : 2 * head]
        qn = lax.rsqrt(row_sum(qp * qp) + NORM_EPS) * scale
        kn = lax.rsqrt(row_sum(kp * kp) + NORM_EPS)
        q = qp * qn
        k = kp * kn
        beta = 1.0 / (1.0 + jnp.exp(-pre[:, 2 * head : 3 * head]))
        x = pre[:, 3 * head :] + bias
        g = rate * (jnp.maximum(x, 0.0) + jnp.log1p(jnp.exp(-jnp.abs(x))))
        g1 = g.astype(BF16)
        g2, g3 = halves(g - g1.astype(F32))
        split = cut(jnp.concatenate([g1, g2, g3], 1))
        sums = [nn(low_ones, split[i]) for i in each]
        cs = [s[:, :head] + (s[:, head : 2 * head] + s[:, 2 * head :]) for s in sums]
        lasts = [c[CHUNK - 1 : CHUNK, :] for c in cs]
        e = jnp.exp(join(cs))
        tail = jnp.exp(join([last - c for last, c in zip(lasts, cs)]))
        gam = jnp.exp(join([jnp.where(low, c - c.T, -1e30) for c in cs]))
        kpair = halves(k)
        khigh, klow = cut(kpair[0]), cut(kpair[1])
        q16 = cut(q.astype(BF16))
        kk = join([fine_gram((khigh[i], klow[i])) for i in each])
        qk = join([nt(q16[i], khigh[i]) for i in each])
        strict_all, low_all = join([strict] * group), join([low] * group)
        mats = cut(jnp.where(strict_all, beta * gam * kk, 0.0))
        p_all = (gam * qk).astype(BF16)
        kt_all = (tail * k).astype(BF16)
        ek_bv = cut(jnp.concatenate([beta * e * k, beta * v], 1))
        p, kt, eq = cut(p_all), cut(kt_all), cut(e * q)
        for ref, value in (
            (kk_s, kk), (qk_s, qk), (q_s, q), (k_s, k), (b_s, beta), (e_s, e), (tail_s, tail), (gam_s, gam), (x_s, x),
            (p_s, p_all), (kt_s, kt_all),
            (qn_s, jnp.broadcast_to(qn, q.shape)), (kn_s, jnp.broadcast_to(kn, q.shape)),
        ):
            ref[here, :] = value
        for i in each:
            ec_s[first + i] = jnp.exp(jnp.broadcast_to(lasts[i], (8, head)))
        eye = jnp.where(row_id == col_id, 1.0, 0.0)
        inv = [eye - jnp.where((row_id >> 1) == (col_id >> 1), a, 0.0) for a in mats]
        pairs = [halves(a) for a in mats]
        level = 1
        while (2 << level) <= CHUNK:
            wide = (4 << level) <= CHUNK
            reach = level + (2 if wide else 1)
            joint = ((row_id >> reach) == (col_id >> reach)) & ((row_id >> level) > (col_id >> level))
            tp = [halves(t) for t in inv]
            left = [
                halves(fine_nn(tp[i], tuple(jnp.where(joint, half, jnp.zeros_like(half)) for half in pairs[i])))
                for i in each
            ]
            inv = [inv[i] - fine_nn(left[i], tp[i]) for i in each]
            if wide:
                square = [halves(fine_nn(z, z)) for z in left]
                inv = [inv[i] + fine_nn(square[i], halves(inv[i])) for i in each]
            level = reach
        tp = [halves(t) for t in inv]
        ep = [halves(y) for y in ek_bv]
        wu = [
            nn(jnp.concatenate(tp[i], 1), jnp.concatenate([ep[i][0], ep[i][0]], 0)) + nn(tp[i][0], ep[i][1])
            for i in each
        ]
        w = [y[:, :head].astype(BF16) for y in wu]
        fg = [tn(kt[i], jnp.concatenate([w[i], wu[i][:, head:].astype(BF16)], 1)) for i in each]
        pw = [nn(p[i], w[i]) for i in each]
        hs = [tn((eq[i] - pw[i]).astype(BF16), cot_ref[spans[i], :]) for i in each]
        t_s[here, :] = join([t[0] for t in tp])
        w_s[here, :] = join(w)
        u0_s[here, :] = join([y[:, head:] for y in wu])
        f_s[here, :] = join([y[:, :head].astype(BF16) for y in fg])
        g_s[here, :] = join([y[:, head:] for y in fg])
        h_s[here, :] = join(hs)

    loop(prepare)

    m_s[pl.ds(0, head), :] = jnp.zeros((head, head), F32)
    d_s[pl.ds((num - 1) * head, head), :] = jnp.zeros((head, head), F32)
    m = jnp.zeros((head, head), F32)
    d = jnp.zeros((head, head), F32)
    for i in range(num):
        span = pl.ds(i * CHUNK, CHUNK)
        if i == 0:
            m = g_s[span, :]
        else:
            m = ec_s[i][:1] * m - nn(f_s[span, :], m.astype(BF16)) + g_s[span, :]
        m_s[pl.ds((i + 1) * head, head), :] = m
        r = num - 1 - i
        if r > 0:
            back = pl.ds(r * CHUNK, CHUNK)
            if r == num - 1:
                d = h_s[back, :]
            else:
                d = ec_s[r][:1] * d - tn(f_s[back, :], d.astype(BF16)) + h_s[back, :]
            d_s[pl.ds((r - 1) * head, head), :] = d

    def finish(first):
        here = rows_of(first)
        q, k, beta = q_s[here, :], k_s[here, :], b_s[here, :]
        gam, e, tail = gam_s[here, :], e_s[here, :], tail_s[here, :]
        do = cot_ref[here, :]
        m32, d32 = m_s[here, :], d_s[here, :]
        m, d = cut(m32.astype(BF16)), cut(d32.astype(BF16))
        q16, k16 = q.astype(BF16), k.astype(BF16)
        k_parts, qk_parts = cut(k16), [join([a, b]) for a, b in zip(cut(q16), cut(-k16))]
        p, kt, t, w, dos = cut(p_s[here, :]), cut(kt_s[here, :]), cut(t_s[here, :]), cut(w_s[here, :]), cut(do)
        strict_all = join([strict] * group)
        du = [tn(p[i], dos[i]) + nn(kt[i], d[i]) for i in each]
        u = u0_s[here, :] - join([nn(w[i], m[i]) for i in each])
        u16 = cut(u.astype(BF16))
        dr = join([tn(t[i], du[i].astype(BF16)) for i in each])
        dv = beta * dr
        dv16 = dv.astype(BF16)
        dvs = cut(dv16)
        wide = [nt(join([dos[i], dvs[i]]), join([u16[i], m[i]])) for i in each]
        ud = join([nt(u16[i], d[i]) for i in each])
        y32 = join([a[:CHUNK, :CHUNK] for a in wide]) * gam
        x32 = jnp.where(strict_all, join([a[CHUNK:, :CHUNK] for a in wide]) * gam, 0.0)
        yx = [join([a, b]) for a, b in zip(cut(y32.astype(BF16)), cut(x32.astype(BF16)))]
        by_k = [nn(yx[i], k_parts[i]) for i in each]
        by_qk = join([tn(yx[i], qk_parts[i]) for i in each])
        from_q = e * join([a[:CHUNK, CHUNK:] for a in wide])
        from_k = e * join([a[CHUNK:, CHUNK:] for a in wide])
        to_k = tail * ud
        dq = from_q + join([a[:CHUNK] for a in by_k])
        dk = to_k - from_k - join([a[CHUNK:] for a in by_k]) + by_qk
        zc = halves(jnp.where(strict_all, y32 * qk_s[here, :], 0.0) - x32 * kk_s[here, :])
        zr = halves(q * from_q - k * from_k)
        zt = cut(jnp.concatenate(halves(k * to_k), 1))
        zs = cut(jnp.concatenate([*zc, *zr], 1))
        up = join([nn(high_ones, zs[i]) for i in each])
        down = join([nn(below_ones, zt[i]) for i in each])
        crossing = jnp.where(strict_all, up[:, :head] + up[:, head : 2 * head], 0.0)
        single = up[:, 2 * head : 3 * head] + up[:, 3 * head :] + down[:, :head] + down[:, head:]
        carried = join([
            jnp.broadcast_to(row_sum(jnp.sum(ec_s[first + i][:1] * a, axis=0, keepdims=True)), (CHUNK, 1))
            for i, a in enumerate(cut(m32 * d32))
        ])
        dg = row_sum(crossing + single) + carried
        ga = (dg * rate) * (1.0 / (1.0 + jnp.exp(-x_s[here, :])))
        gb = row_sum(dr * u) * (1.0 - beta)
        gq = (qn_s[here, :] * (dq - q * (row_sum(q * dq) * head))).astype(BF16)
        gk = (kn_s[here, :] * (dk - k * row_sum(k * dk))).astype(BF16)
        lane = lax.broadcasted_iota(jnp.int32, q.shape, 1)
        gba = jnp.where(lane == 0, gb, jnp.where(lane == 1, ga, 0.0)).astype(BF16)
        near_ref[here, :] = jnp.concatenate([gq[:, :half], gk[:, :half]], 1)
        away_ref[here, :] = jnp.concatenate([gq[:, half:], gk[:, half:]], 1)
        value_ref[here, :] = dv16
        forth = jnp.concatenate([gq, gk, dv16, gba], 1)
        swapped = jnp.concatenate([gq[:, half:], gq[:, :half], gk[:, half:], gk[:, :half], dv16, gba], 1)
        first_core = core == 0
        pieces = group * CHUNK // (2 * part)
        for j in range(pieces):
            lo = slice(2 * j * part, (2 * j + 1) * part)
            hi = slice((2 * j + 1) * part, (2 * j + 2) * part)
            slot = first * CHUNK // (2 * part) + j
            to = pl.ds(slot * part if isinstance(slot, int) else pl.multiple_of(slot * part, part), part)
            mine_ref[to, :] = jnp.where(first_core, forth[lo], forth[hi])
            theirs_ref[to, :] = jnp.where(first_core, swapped[hi], swapped[lo])

    loop(finish)
    vsum_ref[...] = tn(value_ref[...], rows_ref[...]).astype(BF16)


def core_grads(order, messages, narrow, narrow2, wv, log_rate, rate_bias):
    part, features = messages[0].shape[0], wv.shape[0]
    head = wv.shape[1]
    total = part * len(messages)
    num = total // CHUNK
    col = lambda dt: pltpu.VMEM((total, head), dt)
    states = pltpu.VMEM(((num + 1) * head, head), F32)
    out = lambda rows, cols: jax.ShapeDtypeStruct((rows, cols), BF16)
    args = (*messages, narrow, narrow2, wv, log_rate, rate_bias)
    return pl.pallas_call(
        functools.partial(core_kernel, order),
        out_shape=(
            out(total, features), out(total, head), out(total, head), out(head, features),
            out(total // 2, 4 * head), out(total // 2, 4 * head),
        ),
        in_specs=[pl.BlockSpec(memory_space=pltpu.VMEM)] * len(args),
        out_specs=[pl.BlockSpec(memory_space=pltpu.VMEM)] * 6,
        scratch_shapes=[
            col(BF16), col(BF16), col(F32), col(F32),
            col(F32), col(F32), col(F32), col(F32), col(F32), col(F32), col(BF16), col(BF16), col(BF16), col(F32),
            col(BF16), col(F32), col(F32), col(F32),
            col(BF16), col(F32), col(F32), pltpu.VMEM((num, 8, head), F32), states, states,
        ],
        compiler_params=pltpu.CompilerParams(vmem_limit_bytes=48 * 1024 * 1024),
        name="core_grads",
    )(*args)


def pack_kernel(chips, hidden_ref, cot_ref, *outs):
    chip = lax.axis_index("head") // 2
    width, features = cot_ref.shape[1] // chips, hidden_ref.shape[1]
    for far, out in enumerate(outs):
        out[:, :features] = hidden_ref[...]
        out[:, features:] = cot_ref[:, pl.ds(pl.multiple_of((chip ^ far) * width, width), width)]


def narrow_kernel(wq_ref, wk_ref, wb_ref, wa_ref, after_ref, out_ref):
    half, features = wq_ref.shape
    out_ref[pl.ds(0, half), :] = wq_ref[...]
    out_ref[pl.ds(half, half), :] = wk_ref[...]
    line = lax.broadcasted_iota(jnp.int32, (16, features), 0)
    beta, decay = wb_ref[...].astype(F32), wa_ref[...].astype(F32)
    out_ref[pl.ds(2 * half, 16), :] = jnp.where(line == 0, beta, jnp.where(line == 1, decay, 0.0)).astype(BF16)


def gram_kernel(rows_ref, near_ref, away_ref, out_ref):
    rows = rows_ref[...]
    out_ref[...] = (tn(near_ref[...], rows) + tn(away_ref[...], rows)).astype(BF16)


def term_kernel(part, mine_ref, recv_ref, own, partner, wv_ref, wv2_ref, *outs):
    outs, all_ref = outs[:-1], outs[-1]
    chip = lax.axis_index("head") // 2
    head = wv_ref.shape[1]
    half = head // 2
    narrow = jnp.concatenate([own[:half, :], partner[:half, :], own[half:head, :], partner[half:head, :]], 0)
    small, small2 = own[pl.ds(head, 16), :], partner[pl.ds(head, 16), :]
    mine, recv = mine_ref[...], recv_ref[...]
    both = nn(jnp.concatenate([mine[:, : 2 * head], recv[:, : 2 * head]], 1), jnp.concatenate([narrow, narrow], 0))
    both = both + nt(
        jnp.concatenate([mine[:, 2 * head : 3 * head], recv[:, 2 * head : 3 * head]], 1),
        jnp.concatenate([wv_ref[...], wv2_ref[...]], 1))
    both = both + nn(mine[:, 3 * head : 3 * head + 16], small) + nn(recv[:, 3 * head : 3 * head + 16], small2)
    all_ref[...] = both.astype(BF16)
    for far, out in enumerate(outs):
        out[...] = all_ref[pl.ds(pl.multiple_of((chip ^ far) * part, part), part), :]


def sum_kernel(count, *refs):
    total = refs[0][...].astype(F32)
    for ref in refs[1:count]:
        total = total + ref[...].astype(F32)
    refs[-1][...] = total


def last_kernel(count, own_qk, recv_qk, own_v, recv_v, *refs):
    blocks, (q_ref, k_ref, v_ref, token_ref) = refs[:-4], refs[-4:]
    half = q_ref.shape[0]
    qk = (own_qk[...].astype(F32) + recv_qk[...].astype(F32)) * (1.0 / count)
    q_ref[...] = qk[:half]
    k_ref[...] = qk[half:]
    v_ref[...] = ((own_v[...].astype(F32) + recv_v[...].astype(F32)) * (1.0 / count)).T
    total = blocks[0][...].astype(F32)
    for ref in blocks[1:]:
        total = total + ref[...].astype(F32)
    token_ref[...] = total.astype(BF16)


def add_kernel(own_ref, recv_ref, after_ref, out_ref):
    out_ref[...] = (own_ref[...].astype(F32) + recv_ref[...].astype(F32)).astype(BF16)


def local_call(body, outs, args, name, flops, scratch=(), after=()):
    many = isinstance(outs, tuple)
    spec = pl.BlockSpec(memory_space=pltpu.VMEM)
    return pl.pallas_call(
        body,
        out_shape=outs,
        in_specs=[spec] * len(args) + [pl.BlockSpec(memory_space=pl.ANY)] * len(after),
        out_specs=[spec] * len(outs) if many else spec,
        scratch_shapes=scratch,
        compiler_params=pltpu.CompilerParams(vmem_limit_bytes=48 * 1024 * 1024),
        cost_estimate=pl.CostEstimate(flops=flops, bytes_accessed=1 << 20, transcendentals=0),
        name=name,
    )(*args, *after)


def across(block, distance):
    count = lax.axis_size("head")
    return lax.ppermute(block, "head", [(i, i ^ distance) for i in range(count)])


def across_data(block, step):
    groups, places = lax.axis_size("dp"), lax.axis_size("head")
    bits = groups.bit_length() - 1
    route = []
    for g in range(groups):
        for p in range(places):
            bit = step if p % 2 == 0 else bits - 1 - step
            route.append((g * places + p, (g ^ (1 << bit)) * places + p))
    return lax.ppermute(block, ("dp", "head"), route)


def body(
    hidden, core_grad, query_weight, key_weight, value_weight, beta_weight, decay_weight, decay_log, decay_bias,
):
    half = query_weight.shape[1]
    head = value_weight.shape[1]
    chips = lax.axis_size("head") // 2
    part, features = hidden.shape[1:]
    order = sorted(range(chips), key=lambda d: -d)
    block = lambda rows, dt: jax.ShapeDtypeStruct((rows, features), dt)
    message = jax.ShapeDtypeStruct((part, features + 2 * head), BF16)
    sent = local_call(
        functools.partial(pack_kernel, chips), (message,) * chips, (hidden[0], core_grad[0]), "pack", 1048576)
    got = {d: across(sent[d], 2 * d) if d else sent[0] for d in order}
    narrow = local_call(
        narrow_kernel, block(head + 16, BF16),
        (query_weight.T, key_weight.T, beta_weight.T, decay_weight.T, got[order[0]]), "narrow", 1048576)
    messages = []
    for d in order:
        messages += [got[d], across(got[d], 1)]
    narrow2, wv2 = across(narrow, 1), across(value_weight, 1)

    all_rows, near, away, value, mine, theirs = core_grads(
        order, messages, narrow, narrow2, value_weight, decay_log.reshape(1, 1), decay_bias.reshape(1, 1))
    recv = across(away, 1)
    other = across(theirs, 1)
    qk = local_call(gram_kernel, block(head, BF16), (all_rows, near, recv), "gram", 268435456)
    terms = local_call(
        functools.partial(term_kernel, part), (block(part, BF16),) * chips,
        (mine, other, narrow, narrow2, value_weight, wv2), "terms", 1073741824,
        [pltpu.VMEM((mine.shape[0], features), BF16)],
    )
    received = [across(terms[d], 2 * d) for d in order if d]
    groups = lax.axis_size("dp")
    rounds = groups.bit_length() - 1
    sums = {"value": value, "qk": qk}
    for step in range(rounds - 1):
        for name in sums:
            own = sums[name]
            sums[name] = local_call(add_kernel, block(head, BF16), (own, across_data(own, step), terms[0]), "add", 1048576)
    last = {name: across_data(sums[name], rounds - 1) for name in sums}
    begun = local_call(
        functools.partial(sum_kernel, 2), block(part, F32), (terms[0], received[0]), "token_begin", 17179869184)
    q_mean, k_mean, v_mean, token = local_call(
        functools.partial(last_kernel, groups),
        (block(half, F32), block(half, F32), jax.ShapeDtypeStruct((features, head), F32), block(part, BF16)),
        (sums["qk"], last["qk"], sums["value"], last["value"], begun, *received[1:]), "last", 1048576)
    return token[None], q_mean.T, k_mean.T, v_mean


def solution(mesh):
    rows = P("dp", "head", None)
    cols = P(None, "head")
    return jax.shard_map(
        body,
        mesh=mesh,
        in_specs=(rows, rows, cols, cols, cols, cols, cols, P("head"), P("head")),
        out_specs=(rows, cols, cols, cols),
        check_vma=False,
    )
```
